256 devices in a mesh: wide: 32 (over z_lo, x, core), narrow: 8 (over z_hi, y).
Axes of the slice: x: 4, y: 4, z: 8 (z_hi: 2, z_lo: 4; z = z_hi * 4 + z_lo), core: 2. Of those that a mesh axis runs over, the one named last changes fastest.
Arguments:
- stem: float32 [2, 1, 32, 256, 8, 256], P(None, None, 'wide', None, 'narrow'), may hold values from -6 to 6
- branch_pair: float32 [2, 2, 256, 256], P(None, None, ('wide', 'narrow')), may hold values from -0.25 to 0.25
- branch_last: float32 [2, 256, 256], P(None, 'narrow'), may hold values from -0.25 to 0.25
Outputs:
- absorbed: float32 [2, 1, 32, 256, 8, 256], P(None, None, 'wide', None, 'narrow')
The draws below stay inside these ranges and needn't reach their ends.
All inputs are finite; a program needn't handle non-finite values.
Results may differ from the reference program's by a relative error of at most 0.000098.
Values sent between devices are 32-bit elements; how exact they have to be, the bound alone decides.
A program may use at most 64 MiB of HBM per device.

```python
import jax
import jax.numpy as jnp
from jax import lax

ROWS = 1
GROUP = 256
TAIL = 256
N_WIDE = 32
N_NARROW = 8


def level_of(own_key, dims, shards, low, largest):
    loudness = 1.0
    for axis_at, shards_of in shards:
        draws = jax.random.uniform(jax.random.fold_in(jax.random.fold_in(own_key, 6), axis_at), (shards_of,), jnp.float32, low / len(shards), largest / len(shards))
        loudness = loudness * jnp.repeat(jnp.exp(draws), dims[axis_at] // shards_of).reshape((-1,) + (1,) * (len(dims) - 1 - axis_at))
    return loudness


def centred(key, extent, scale, reach, cuts=(), dtype=jnp.bfloat16):
    factor_of = level_of(key, extent, cuts, -0.22, 0.18) if cuts else 1.0
    drawn = jax.random.normal(key, extent, jnp.float32) * scale * factor_of
    return jnp.minimum(jnp.maximum(drawn, -reach), reach).astype(dtype)


def setup_inputs(seed: int = 0) -> dict:
    splits = jax.random.split(jax.random.key(seed), 4)
    return {
        "stem": centred(splits[0], (2, ROWS, N_WIDE, GROUP, N_NARROW, TAIL), 1.0, 6.0, ((2, 32), (4, 8)), jnp.float32),
        "branch_pair": centred(splits[1], (2, 2, GROUP, GROUP), (2 * GROUP) ** -0.5, 0.25, ((2, 256),), jnp.float32),
        "branch_last": centred(splits[2], (2, TAIL, TAIL), (2 * TAIL) ** -0.5, 0.25, ((1, 8),), jnp.float32),
    }


HIGHEST = lax.Precision.HIGHEST


def complex_apply(form, branch, data):
    def single(matrix, values):
        return jnp.einsum(form, matrix, values, precision=HIGHEST)
    real_part = single(branch[0], data[0]) - single(branch[1], data[1])
    imag_part = single(branch[0], data[1]) + single(branch[1], data[0])
    return jnp.stack([real_part, imag_part])


def absorb_slice(slab, first_branch, third_branch, tail_branch):
    wide_count = N_WIDE
    narrow_count = N_NARROW
    lower_one = GROUP // wide_count
    lower_two = TAIL // narrow_count
    lower_three = GROUP // (wide_count * narrow_count)
    shaped = slab.reshape(2, wide_count, wide_count, lower_one, narrow_count, TAIL)
    matrix = first_branch.reshape(2, wide_count, lower_one, wide_count, lower_one)
    shaped = complex_apply("pqwl,walvh->paqvh", matrix, shaped)
    shaped = shaped.reshape(2, wide_count, GROUP, narrow_count, narrow_count, lower_two)
    matrix = tail_branch.reshape(2, narrow_count, lower_two, narrow_count, lower_two)
    shaped = complex_apply("pqvl,wgval->wgpaq", matrix, shaped)
    shaped = shaped.reshape(2, wide_count, wide_count, narrow_count, lower_three, narrow_count, TAIL)
    matrix = third_branch.reshape(2, wide_count, lower_three, narrow_count, wide_count, lower_three, narrow_count)
    shaped = complex_apply("pqswlv,wablvh->pabqsh", matrix, shaped)
    return shaped.reshape(2, wide_count, GROUP, narrow_count, TAIL)


def reference(stem, branch_pair, branch_last):
    moved = jnp.moveaxis(stem, 1, 0)

    def one_slice(slab):
        return absorb_slice(slab, branch_pair[0], branch_pair[1], branch_last)

    result = lax.map(one_slice, moved)
    return jnp.moveaxis(result, 0, 1)
```

```python
import jax
import jax.numpy as jnp
from jax import lax
from jax.sharding import PartitionSpec as P

PRECISION = lax.Precision.HIGH
BOTH = ("wide", "narrow")


def multiply(form, branch, data):

    def single(matrix, values):
        return jnp.einsum(form, matrix, values, precision=PRECISION)

    real_part = single(branch[0], data[0]) - single(branch[1], data[1])
    imag_part = single(branch[0], data[1]) + single(branch[1], data[0])
    return jnp.stack([real_part, imag_part])


def on_device(stem, branch_pair, branch_last):
    group_size = stem.shape[3]
    tail_size = stem.shape[5]
    wide_count = lax.axis_size("wide")
    narrow_count = lax.axis_size("narrow")
    devices = wide_count * narrow_count
    g_low = group_size // wide_count
    t_low = tail_size // narrow_count

    pair = lax.all_gather(branch_pair, BOTH, axis=2, tiled=True)
    tail = lax.all_gather(branch_last, "narrow", axis=1, tiled=True)

    blocks = stem.reshape(2, wide_count, g_low, narrow_count, t_low)
    blocks = blocks.transpose(1, 3, 0, 2, 4).reshape(devices, -1)
    blocks = lax.all_to_all(blocks, BOTH, split_axis=0, concat_axis=0, tiled=True)
    blocks = blocks.reshape(wide_count, narrow_count, 2, g_low, t_low)
    current = blocks.transpose(2, 0, 3, 1, 4).reshape(2, wide_count * g_low, narrow_count * t_low)
    current = multiply("kj,jh->kh", pair[0], current)
    current = multiply("kj,gj->gk", tail, current)
    current = current.reshape(2, wide_count, g_low, narrow_count, t_low)
    current = current.transpose(0, 1, 3, 2, 4).reshape(2, devices, g_low * t_low)
    current = multiply("kj,jh->kh", pair[1], current)
    blocks = current.transpose(1, 0, 2).reshape(devices, -1)
    blocks = lax.all_to_all(blocks, BOTH, split_axis=0, concat_axis=0, tiled=True)
    blocks = blocks.reshape(wide_count, narrow_count, 2, g_low, t_low)
    return blocks.transpose(2, 0, 3, 1, 4).reshape(stem.shape)


def solution(mesh):
    in_specs = (
        P(None, None, "wide", None, "narrow", None),
        P(None, None, ("wide", "narrow"), None),
        P(None, "narrow", None),
    )
    out_specs = P(None, None, "wide", None, "narrow", None)
    return jax.shard_map(
        on_device, mesh=mesh, in_specs=in_specs, out_specs=out_specs, check_vma=False
    )
```

```python
import functools

import jax
import jax.numpy as jnp
from jax import lax
from jax.experimental import pallas as pl
from jax.experimental.pallas import tpu as pltpu
from jax.sharding import PartitionSpec as P

MESH = pl.DeviceIdType.MESH
F32 = jnp.float32
BF16 = jnp.bfloat16


def rows(start, count=8):
    return pl.ds(pl.multiple_of(start, 8), count)


def device(z, y, x, core):
    return ((z & 3) * 8 + x * 2 + core, (z >> 2) * 4 + y)


def swap_blocks(tiles):
    lane = lax.broadcasted_iota(jnp.int32, tiles[0].shape, 1)
    low64 = lane < 64
    low32 = (lane & 32) == 0

    def halves(a, b):
        r = pltpu.roll(jnp.where(low64, b, a), 64, 1)
        return jnp.where(low64, a, r), jnp.where(low64, r, b)

    def quarters(a, b):
        return (
            jnp.where(low32, a, pltpu.roll(b, 32, 1)),
            jnp.where(low32, pltpu.roll(a, 96, 1), b),
        )

    a0, a2 = halves(tiles[0], tiles[2])
    a1, a3 = halves(tiles[1], tiles[3])
    return (*quarters(a0, a1), *quarters(a2, a3))


def split(values):
    high = values.astype(BF16)
    return high, (values - high.astype(F32)).astype(BF16)


def dot(a, b):
    return jnp.dot(a, b, preferred_element_type=F32)


def product(ar, ai, br, bi):
    def left(v):
        return jnp.concatenate([v[0], v[0], v[1]], axis=1)

    def right(v):
        return jnp.concatenate([v[0], v[1], v[0]], axis=0)

    lr, li, rr, ri = left(ar), left(ai), right(br), right(bi)
    return dot(lr, rr) - dot(li, ri), dot(lr, ri) + dot(li, rr)


def kernel(
    stem,
    pair,
    tail,
    out,
    xr,
    sent,
    got,
    ga,
    gb,
    wh,
    wl,
    x1,
    y2,
    zz,
    back,
    home,
    final,
    plane_sem,
    local_sem,
    pair_send,
    pair_recv,
    z_send,
    z_recv,
    ring_send,
    ring_recv,
    core_send,
    core_recv,
    go_send,
    go_recv,
    back_send,
    back_recv,
    out_send,
    out_recv,
):
    wide, narrow = lax.axis_index("wide"), lax.axis_index("narrow")
    core, x = wide & 1, (wide >> 1) & 3
    z, y = (narrow >> 2) * 4 + (wide >> 3), narrow & 3
    other = 1 - core
    sibling = device(z, y, x, other)

    def at_z(d):
        return (z + d) & 7

    def at_x(d):
        return (x + d) & 3

    def at_y(d):
        return (y + d) & 3

    def own_half(c):
        return pltpu.make_async_copy(
            stem.at[rows(c * 512 + core * 256, 256)],
            xr.at[rows(core * 512 + c * 256, 256)],
            local_sem.at[c],
        )

    for c in range(2):
        own_half(c).start()

    barrier = pltpu.get_barrier_semaphore()
    pl.semaphore_signal(barrier, inc=1, device_id=sibling, device_id_type=MESH)
    for d in range(1, 8):
        pl.semaphore_signal(barrier, inc=1, device_id=device(at_z(d), y, x, core), device_id_type=MESH)
    for d in range(1, 16):
        pl.semaphore_signal(
            barrier, inc=1, device_id=device(z, at_y(d // 4), at_x(d % 4), core), device_id_type=MESH
        )

    slot_a = ((core * 4 + y) * 8 + z) * 4 + x
    slot_b = ((core * 4 + x) * 8 + z) * 4 + y
    ga[rows(slot_a * 8), :] = pair[...]
    line = lax.broadcasted_iota(jnp.int32, (8, 128), 0)
    pieces = []
    for c in range(2):
        for h in range(2):
            tile = tail[c, rows((z & 3) * 8), h * 128 : h * 128 + 128]
            pieces.append(jnp.sum(jnp.where(line == core * 4 + x, tile, 0.0), axis=0, keepdims=True))
    gb[rows(slot_b * 8), :] = jnp.concatenate([*pieces, jnp.zeros((4, 128), F32)], axis=0)

    pl.semaphore_wait(barrier, 23)

    for d in range(1, 8):
        pl.semaphore_signal(plane_sem, inc=1, device_id=device(at_z(d), y, x, core), device_id_type=MESH)

    def half_across(c):
        return pltpu.make_async_remote_copy(
            stem.at[rows(c * 512 + other * 256, 256)],
            xr.at[rows(core * 512 + c * 256, 256)],
            pair_send.at[c],
            pair_recv.at[c],
            device_id=sibling,
            device_id_type=MESH,
        )

    for c in range(2):
        half_across(c).start()

    def along_z(buffer, which, slot, d):
        return pltpu.make_async_remote_copy(
            buffer.at[rows(slot * 8)],
            buffer.at[rows(slot * 8)],
            z_send.at[which],
            z_recv.at[which],
            device_id=device(at_z(d), y, x, core),
            device_id_type=MESH,
        )

    for d in (4, 3, 5, 2, 6, 1, 7):
        along_z(ga, 0, slot_a, d).start()
        along_z(gb, 1, slot_b, d).start()

    for c in range(2):
        own_half(c).wait()
    for c in range(2):
        half_across(c).wait()
    pl.semaphore_wait(plane_sem, 7)

    def block_ax(p):
        return lambda lo, n: ga.reshape(2, 4, 8, 4, 8, 128).at[core, y, pl.ds(lo, n), p]

    def block_by(p):
        return lambda lo, n: gb.reshape(2, 4, 8, 4, 8, 128).at[core, x, pl.ds(lo, n), p]

    def block_ay(p):
        return lambda lo, n: ga.reshape(2, 4, 8, 4, 8, 128).at[core, p, pl.ds(lo, n)]

    def block_bx(p):
        return lambda lo, n: gb.reshape(2, 4, 8, 4, 8, 128).at[core, p, pl.ds(lo, n)]

    def on_x(d):
        return at_x(d), device(z, y, at_x(d), core)

    def on_y(d):
        return at_y(d), device(z, at_y(d), x, core)

    def ring_copy(number, block, step, place, lo, n):
        holder = place(0)[0] if step < 2 else place(-1 if step == 2 else 1)[0]
        ref = block(holder)(lo, n)
        return pltpu.make_async_remote_copy(
            ref,
            ref,
            ring_send.at[number, step],
            ring_recv.at[number, step],
            device_id=place(1 if step in (0, 2) else -1)[1],
            device_id_type=MESH,
        )

    def ring(number, block, place):
        copies = [
            ring_copy(number, block, 0, place, 0, 8),
            ring_copy(number, block, 1, place, 0, 8),
            ring_copy(number, block, 2, place, 0, 4),
            ring_copy(number, block, 3, place, 4, 4),
        ]

        def start():
            copies[0].start()
            copies[1].start()

        def forward():
            copies[0].wait_recv()
            copies[2].start()
            copies[1].wait_recv()
            copies[3].start()

        def finish():
            copies[2].wait_recv()
            copies[3].wait_recv()

        def drain():
            for copy in copies:
                copy.wait_send()

        return start, forward, finish, drain

    rings = [
        ring(0, block_ax, on_x),
        ring(1, block_by, on_y),
        ring(2, block_ay, on_y),
        ring(3, block_bx, on_x),
    ]

    here = (((z & 3) * 4 + x) * 2 + (z >> 2)) * 4 + y

    def shuffle_group(number, zt, xt):
        base = ((zt & 3) * 4 + xt) * 16 + (zt >> 2)
        tiles = [xr[pl.ds(i * 256 + base, 8, stride=2), :] for i in range(4)]
        for j, tile in enumerate(swap_blocks(tiles)):
            sent[rows((number * 4 + j) * 8), :] = tile

    def send_tile(number, zt, yt, xt):
        pltpu.make_async_remote_copy(
            sent.at[rows((number * 4 + yt) * 8)],
            got.at[rows(here * 8)],
            go_send,
            go_recv,
            device_id=device(zt, yt, xt, core),
            device_id_type=MESH,
        ).start()

    def send_groups(dx, dzs):
        for dz in dzs:
            zt, xt = at_z(dz), at_x(dx)
            number = dx * 8 + dz
            shuffle_group(number, zt, xt)
            for dy in range(4):
                send_tile(number, zt, at_y(dy), xt)

    send_groups(0, (4, 3, 5, 2, 6, 1, 7))
    part = rows(0, 56)
    for which, buffer in ((0, ga), (1, gb)):
        pltpu.make_async_copy(buffer.at[part], buffer.at[part], z_recv.at[which]).wait()
    rings[0][0]()
    rings[1][0]()
    send_groups(1, (4, 3, 5, 2, 6, 1, 7, 0))
    rings[0][1]()
    rings[1][1]()
    send_groups(2, (4, 3, 5, 2, 6, 1, 7, 0))
    rings[0][2]()
    rings[1][2]()
    rings[2][0]()
    rings[3][0]()
    send_groups(3, (4, 3, 5, 2, 6, 1, 7, 0))
    shuffle_group(0, z, x)
    for dy in range(1, 4):
        send_tile(0, z, at_y(dy), x)
    got[rows(here * 8), :] = sent[rows(y * 8), :]
    rings[2][1]()
    rings[3][1]()
    rings[2][2]()
    rings[3][2]()

    def core_copy(which, buffer):
        ref = buffer.at[rows(core * 1024, 1024)]
        return pltpu.make_async_remote_copy(
            ref, ref, core_send.at[which], core_recv.at[which], device_id=sibling, device_id_type=MESH
        )

    core_copy(0, ga).start()
    core_copy(1, gb).start()
    core_copy(0, ga).wait_recv()
    core_copy(1, gb).wait_recv()

    def weights(step, c):
        halves = []
        for h in range(2):
            k = step * 4 + c * 2 + h
            halves.append(jnp.concatenate([ga[pl.ds(i * 64 + k, 8, stride=8), :] for i in range(32)], axis=0))
        return jnp.concatenate(halves, axis=1)

    def tail_weights(c):
        halves = []
        for h in range(2):
            k = c * 2 + h
            blocks = []
            for i in range(32):
                zi, yi = (i // 16) * 4 + i % 4, (i // 4) % 4
                blocks.append(gb[pl.ds((zi * 4 + yi) * 8 + k, 8, stride=256), :])
            halves.append(jnp.concatenate(blocks, axis=0))
        return jnp.concatenate(halves, axis=1)

    for c in range(2):
        for step in range(2):
            wh[step, c], wl[step, c] = split(weights(step, c))
        wh[2, c], wl[2, c] = split(tail_weights(c).T)

    part = rows(0, 127 * 8)
    pltpu.make_async_copy(got.at[part], got.at[part], go_recv).wait()

    @pl.loop(0, 16)
    def _(i):
        for h in range(2):
            tiles = [got[rows((i * 8 + h * 4 + j) * 8), :] for j in range(4)]
            for k, tile in enumerate(swap_blocks(tiles)):
                x1[k % 2, rows(i * 16 + (k // 2) * 8), h * 128 : h * 128 + 128] = tile

    def weight(number, c):
        return wh[number, c], wl[number, c]

    first = product(weight(0, 0), weight(0, 1), split(x1[0]), split(x1[1]))
    second = product(split(first[0]), split(first[1]), weight(2, 0), weight(2, 1))
    y2[0] = second[0]
    y2[1] = second[1]
    for c in range(2):
        for k in range(2):
            for h in range(2):
                for vh in range(2):
                    for jb in range(2):
                        tiles = [
                            y2[c, rows(k * 128 + j * 32 + h * 16 + jb * 8), vh * 128 : vh * 128 + 128] for j in range(4)
                        ]
                        for j, tile in enumerate(swap_blocks(tiles)):
                            zz[c * 2 + h, pl.ds(jb * 128 + k * 8 + vh * 4 + j, 8, stride=16), :] = tile

    def contracted(c):
        return split(jnp.concatenate([zz[c * 2], zz[c * 2 + 1]], axis=1))

    third = product(weight(1, 0), weight(1, 1), contracted(0), contracted(1))
    for c in range(2):
        for k in range(2):
            for h in range(2):
                for i in range(16):
                    back[pl.ds(i * 64 + h * 4 + k * 2 + c, 8, stride=8), :] = third[c][
                        k * 128 + i * 8 : k * 128 + i * 8 + 8, h * 128 : h * 128 + 128
                    ]

    there = (z * 4 + x) * 4 + y

    def send_back(zt, yt, xt):
        pltpu.make_async_remote_copy(
            back.at[rows(((yt * 8 + zt) * 4 + xt) * 8)],
            home.at[rows(there * 8)],
            back_send,
            back_recv,
            device_id=device(zt, yt, xt, core),
            device_id_type=MESH,
        ).start()

    @pl.loop(0, 16)
    def _(i):
        for dz in (4, 3, 5, 2, 6, 1, 7):
            send_back(at_z(dz), at_y(i & 3), at_x(i >> 2))

        @pl.when(i > 0)
        def _():
            send_back(z, at_y(i & 3), at_x(i >> 2))

    home[rows(there * 8), :] = back[rows(((y * 8 + z) * 4 + x) * 8), :]
    part = rows(0, 127 * 8)
    pltpu.make_async_copy(home.at[part], home.at[part], back_recv).wait()

    @pl.loop(0, 16)
    def _(i):
        for h in range(2):
            group = h * 16 + i
            tiles = [home[rows((group * 4 + j) * 8), :] for j in range(4)]
            for j, tile in enumerate(swap_blocks(tiles)):
                for gh in range(2):
                    final[pl.ds(i * 16 + (gh * 4 + j) * 2 + h, 4, stride=256), :] = tile[gh * 4 : gh * 4 + 4]

    def out_here(c):
        return pltpu.make_async_copy(
            final.at[rows(core * 512 + c * 256, 256)], out.at[rows(c * 512 + core * 256, 256)], local_sem.at[c]
        )

    def out_across(c):
        return pltpu.make_async_remote_copy(
            final.at[rows(other * 512 + c * 256, 256)],
            out.at[rows(c * 512 + core * 256, 256)],
            out_send.at[c],
            out_recv.at[c],
            device_id=sibling,
            device_id_type=MESH,
        )

    for c in range(2):
        out_across(c).start()
        out_here(c).start()

    for which, buffer in ((0, ga), (1, gb)):
        core_copy(which, buffer).wait_send()
        pltpu.make_async_copy(buffer.at[rows(0, 56)], buffer.at[rows(0, 56)], z_send.at[which]).wait()
    for one in rings:
        one[3]()
    pltpu.make_async_copy(sent.at[part], sent.at[part], go_send).wait()
    pltpu.make_async_copy(back.at[part], back.at[part], back_send).wait()
    for c in range(2):
        out_here(c).wait()
        out_across(c).wait()


def on_device(stem, branch_pair, branch_last):
    dma = pltpu.SemaphoreType.DMA
    whole = pltpu.VMEM((1024, 128), F32)
    result = pl.pallas_call(
        kernel,
        out_shape=jax.ShapeDtypeStruct((1024, 128), F32),
        in_specs=[
            pl.BlockSpec(memory_space=pl.ANY),
            pl.BlockSpec(memory_space=pltpu.VMEM),
            pl.BlockSpec(memory_space=pltpu.VMEM),
        ],
        out_specs=pl.BlockSpec(memory_space=pl.ANY),
        scratch_shapes=[
            whole,
            whole,
            whole,
            pltpu.VMEM((2048, 128), F32),
            pltpu.VMEM((2048, 128), F32),
            pltpu.VMEM((3, 2, 256, 256), BF16),
            pltpu.VMEM((3, 2, 256, 256), BF16),
            pltpu.VMEM((2, 256, 256), F32),
            pltpu.VMEM((2, 256, 256), F32),
            pltpu.VMEM((4, 256, 128), F32),
            whole,
            whole,
            whole,
            pltpu.SemaphoreType.REGULAR,
            dma((2,)),
            dma((2,)),
            dma((2,)),
            dma((2,)),
            dma((2,)),
            dma((4, 4)),
            dma((4, 4)),
            dma((2,)),
            dma((2,)),
            dma,
            dma,
            dma,
            dma,
            dma((2,)),
            dma((2,)),
        ],
        compiler_params=pltpu.CompilerParams(collective_id=0, has_side_effects=True, vmem_limit_bytes=40 << 20),
        name="absorb",
    )(stem.reshape(1024, 128), branch_pair.reshape(8, 128), branch_last)
    return result.reshape(stem.shape)


def solution(mesh):
    in_specs = (
        P(None, None, "wide", None, "narrow", None),
        P(None, None, ("wide", "narrow"), None),
        P(None, "narrow", None),
    )
    out_specs = P(None, None, "wide", None, "narrow", None)
    return jax.shard_map(on_device, mesh=mesh, in_specs=in_specs, out_specs=out_specs, check_vma=False)
```

```python
import functools

import jax
import jax.numpy as jnp
from jax import lax
from jax.experimental import pallas as pl
from jax.experimental.pallas import tpu as pltpu
from jax.sharding import PartitionSpec as P

MESH = pl.DeviceIdType.MESH
F32 = jnp.float32
BF16 = jnp.bfloat16
ORDER = ("z", "r0", "h", "t0", "r1", "r2", "t1", "t2", "t3", "t4", "r3", "g", "c")


def rows(start, count=8):
    return pl.ds(start if isinstance(start, int) else pl.multiple_of(start, 8), count)


def device(z, y, x, core):
    return ((z & 3) * 8 + x * 2 + core, (z >> 2) * 4 + y)


def swap_blocks(tiles):
    lane = lax.broadcasted_iota(jnp.int32, tiles[0].shape, 1)
    low64 = lane < 64
    low32 = (lane & 32) == 0

    def halves(a, b):
        r = pltpu.roll(jnp.where(low64, b, a), 64, 1)
        return jnp.where(low64, a, r), jnp.where(low64, r, b)

    def quarters(a, b):
        return (
            jnp.where(low32, a, pltpu.roll(b, 32, 1)),
            jnp.where(low32, pltpu.roll(a, 96, 1), b),
        )

    a0, a2 = halves(tiles[0], tiles[2])
    a1, a3 = halves(tiles[1], tiles[3])
    return (*quarters(a0, a1), *quarters(a2, a3))


def split(values):
    high = values.astype(BF16)
    return high, (values - high.astype(F32)).astype(BF16)


def dot(a, b):
    return jnp.dot(a, b, preferred_element_type=F32)


def product(ar, ai, br, bi):
    def left(v):
        return jnp.concatenate([v[0], v[0], v[1]], axis=1)

    def right(v):
        return jnp.concatenate([v[0], v[1], v[0]], axis=0)

    lr, li, rr, ri = left(ar), left(ai), right(br), right(bi)
    return dot(lr, rr) - dot(li, ri), dot(lr, ri) + dot(li, rr)


def kernel(
    stem,
    pair,
    tail,
    out,
    xr,
    sent,
    got,
    tails,
    ga,
    gb,
    wh,
    wl,
    x1,
    y2,
    zz,
    back,
    home,
    final,
    plane_sem,
    local_sem,
    branch_sem,
    pair_send,
    pair_recv,
    z_send,
    z_recv,
    ring_send,
    ring_recv,
    core_send,
    core_recv,
    go_send,
    go_recv,
    back_send,
    back_recv,
    out_send,
    out_recv,
):
    wide, narrow = lax.axis_index("wide"), lax.axis_index("narrow")
    core, x = wide & 1, (wide >> 1) & 3
    z, y = (narrow >> 2) * 4 + (wide >> 3), narrow & 3
    other = 1 - core
    sibling = device(z, y, x, other)

    def at_z(d):
        return (z + d) & 7

    def at_x(d):
        return (x + d) & 3

    def at_y(d):
        return (y + d) & 3

    def own_half(c):
        return pltpu.make_async_copy(
            stem.at[rows(c * 512 + core * 256, 256)],
            xr.at[rows(core * 512 + c * 256, 256)],
            local_sem.at[c],
        )

    barrier = pltpu.get_barrier_semaphore()
    for d in range(1, 16):
        pl.semaphore_signal(
            barrier, inc=1, device_id=device(z, at_y(d // 4), at_x(d % 4), core), device_id_type=MESH
        )
    for d in range(1, 8):
        pl.semaphore_signal(barrier, inc=1, device_id=device(at_z(d), y, x, core), device_id_type=MESH)
    pl.semaphore_signal(barrier, inc=1, device_id=sibling, device_id_type=MESH)

    slot_a = ((core * 4 + y) * 8 + z) * 4 + x
    slot_b = (z * 4 + x) * 4 + y
    fetches = [
        pltpu.make_async_copy(tail, tails, branch_sem.at[0]),
        pltpu.make_async_copy(pair, ga.at[rows(slot_a * 8)], branch_sem.at[1]),
    ]
    for fetch in fetches:
        fetch.start()
    for c in range(2):
        own_half(c).start()

    for fetch in fetches:
        fetch.wait()
    gathers_tail = (z >> 2) == core

    @pl.when(gathers_tail)
    def _():
        line = lax.broadcasted_iota(jnp.int32, (8, 128), 0)
        pieces = []
        for f in range(2):
            for c in range(2):
                for h in range(2):
                    tile = tails[c, rows(f * 16 + ((z >> 1) & 1) * 8), h * 128 : h * 128 + 128]
                    tile = jnp.where(line == (z & 1) * 4 + x, tile, 0.0)
                    pieces.append(jnp.sum(tile, axis=0, keepdims=True))
        gb[rows(slot_b * 8), :] = jnp.concatenate(pieces, axis=0)

    pl.semaphore_wait(barrier, 23)

    for d in range(1, 8):
        pl.semaphore_signal(plane_sem, inc=1, device_id=device(at_z(d), y, x, core), device_id_type=MESH)

    def half_across(c):
        return pltpu.make_async_remote_copy(
            stem.at[rows(c * 512 + other * 256, 256)],
            xr.at[rows(core * 512 + c * 256, 256)],
            pair_send.at[c],
            pair_recv.at[c],
            device_id=sibling,
            device_id_type=MESH,
        )

    for c in range(2):
        half_across(c).start()

    def along_z(buffer, which, slot, d):
        return pltpu.make_async_remote_copy(
            buffer.at[rows(slot * 8)],
            buffer.at[rows(slot * 8)],
            z_send.at[which],
            z_recv.at[which],
            device_id=device(at_z(d), y, x, core),
            device_id_type=MESH,
        )

    for d in (4, 3, 5, 2, 6, 1, 7):
        along_z(ga, 0, slot_a, d).start()

    @pl.when(gathers_tail)
    def _():
        for d in (4, 3, 5, 2, 6, 1, 7):
            along_z(gb, 1, slot_b, d).start()

    pairs = ga.reshape(2, 4, 2, 4, 4, 8, 128)
    rests = gb.reshape(2, 2, 2, 4, 4, 8, 128)

    def on_x(d):
        return at_x(d), device(z, y, at_x(d), core)

    def on_y(d):
        return at_y(d), device(z, at_y(d), x, core)

    def across(which, ref):
        return pltpu.make_async_remote_copy(
            ref, ref, core_send.at[which], core_recv.at[which], device_id=sibling, device_id_type=MESH
        )

    def ring(number, block, place, which=None):
        def copy(d, holder):
            ref = block(place(holder)[0])
            return pltpu.make_async_remote_copy(
                ref,
                ref,
                ring_send.at[number, d - 1],
                ring_recv.at[number, d - 1],
                device_id=place(d)[1],
                device_id_type=MESH,
            )

        def pass_on(holder):
            if which is not None:
                across(which, block(place(holder)[0])).start()

        def start():
            for d in (2, 1, 3):
                copy(d, 0).start()
            pass_on(0)

        def arrive():
            for d in (1, 3, 2):
                copy(d, -d).wait_recv()
                pass_on(-d)

        def drain():
            for d in (1, 2, 3):
                copy(d, 0).wait_send()

        return start, arrive, drain

    rings = [
        ring(0, lambda p: pairs.at[core, y, 0, :, p], on_x),
        ring(1, lambda p: pairs.at[core, p, 1, :, x], on_y),
        ring(2, lambda p: rests.at[core, 0, :, p, y], on_x),
        ring(3, lambda p: rests.at[core, 1, :, x, p], on_y),
        ring(4, lambda p: pairs.at[core, p, 0], on_y, 0),
        ring(5, lambda p: pairs.at[core, :, 1, :, p], on_x, 0),
        ring(6, lambda p: rests.at[core, 0, :, :, p], on_y, 1),
        ring(7, lambda p: rests.at[core, 1, :, p], on_x, 1),
    ]

    here = (((z & 3) * 4 + x) * 2 + (z >> 2)) * 4 + y

    def shuffle_group(number, zt, xt):
        base = ((zt & 3) * 4 + xt) * 16 + (zt >> 2)
        tiles = [xr[pl.ds(i * 256 + base, 8, stride=2), :] for i in range(4)]
        for j, tile in enumerate(swap_blocks(tiles)):
            sent[rows((number * 4 + j) * 8), :] = tile

    def send_tile(number, zt, yt, xt):
        pltpu.make_async_remote_copy(
            sent.at[rows((number * 4 + yt) * 8)],
            got.at[rows(here * 8)],
            go_send,
            go_recv,
            device_id=device(zt, yt, xt, core),
            device_id_type=MESH,
        ).start()

    def send_groups(dx, dzs):
        for dz in dzs:
            zt, xt = at_z(dz), at_x(dx)
            number = dx * 8 + dz
            shuffle_group(number, zt, xt)
            for dy in range(4):
                send_tile(number, zt, at_y(dy), xt)

    def wait_z():
        part = rows(0, 56)
        pltpu.make_async_copy(ga.at[part], ga.at[part], z_recv.at[0]).wait()

        def wait_tail(count):
            part = rows(0, count * 8)
            pltpu.make_async_copy(gb.at[part], gb.at[part], z_recv.at[1]).wait()

        @pl.when(gathers_tail)
        def _():
            wait_tail(3)

        @pl.when(jnp.logical_not(gathers_tail))
        def _():
            wait_tail(4)

    def wait_halves():
        for c in range(2):
            own_half(c).wait()
        for c in range(2):
            half_across(c).wait()
        pl.semaphore_wait(plane_sem, 7)

    def both(first, step):
        for one in rings[first : first + 4]:
            one[step]()

    def tiles_near():
        send_groups(0, (4, 3, 5, 2, 6, 1, 7))

    def tiles_at(dx):
        send_groups(dx, (4, 3, 5, 2, 6, 1, 7, 0))

    def tiles_here():
        shuffle_group(0, z, x)
        for dy in range(1, 4):
            send_tile(0, z, at_y(dy), x)
        got[rows(here * 8), :] = sent[rows(y * 8), :]

    def wait_across():
        half_a, half_b = rows(other * 1024, 1024), rows(other * 512, 512)
        pltpu.make_async_copy(ga.at[half_a], ga.at[half_a], core_recv.at[0]).wait()
        pltpu.make_async_copy(gb.at[half_b], gb.at[half_b], core_recv.at[1]).wait()

    def arrived():
        part = rows(0, 127 * 8)
        pltpu.make_async_copy(got.at[part], got.at[part], go_recv).wait()

        for i in range(16):
            for h in range(2):
                tiles = [got[rows((i * 8 + h * 4 + j) * 8), :] for j in range(4)]
                for k, tile in enumerate(swap_blocks(tiles)):
                    x1[k % 2, rows(i * 16 + (k // 2) * 8), h * 128 : h * 128 + 128] = tile

    steps = dict(
        g=arrived,
        z=wait_z,
        h=wait_halves,
        t0=tiles_near,
        t1=functools.partial(tiles_at, 1),
        t2=functools.partial(tiles_at, 2),
        t3=functools.partial(tiles_at, 3),
        t4=tiles_here,
        r0=functools.partial(both, 0, 0),
        r1=functools.partial(both, 0, 1),
        r2=functools.partial(both, 4, 0),
        r3=functools.partial(both, 4, 1),
        c=wait_across,
    )
    for step in ORDER:
        steps[step]()

    def weights(step, c):
        halves = []
        for h in range(2):
            k = step * 4 + c * 2 + h
            halves.append(jnp.concatenate([ga[pl.ds(i * 64 + k, 8, stride=8), :] for i in range(32)], axis=0))
        return jnp.concatenate(halves, axis=1)

    def tail_weights(c):
        halves = []
        for h in range(2):
            blocks = []
            for n in range(8):
                for f in range(2):
                    for j in range(2):
                        start = ((n // 4) * 64 + j * 32 + n % 4) * 8 + f * 4 + c * 2 + h
                        blocks.append(gb[pl.ds(start, 8, stride=32), :])
            halves.append(jnp.concatenate(blocks, axis=0))
        return jnp.concatenate(halves, axis=1)

    for c in range(2):
        for step in range(2):
            wh[step, c], wl[step, c] = split(weights(step, c))
        wh[2, c], wl[2, c] = split(tail_weights(c).T)

    def weight(number, c):
        return wh[number, c], wl[number, c]

    first = product(weight(0, 0), weight(0, 1), split(x1[0]), split(x1[1]))
    second = product(split(first[0]), split(first[1]), weight(2, 0), weight(2, 1))
    y2[0] = second[0]
    y2[1] = second[1]
    for c in range(2):
        for k in range(2):
            for h in range(2):
                for vh in range(2):
                    for jb in range(2):
                        tiles = [
                            y2[c, rows(k * 128 + j * 32 + h * 16 + jb * 8), vh * 128 : vh * 128 + 128] for j in range(4)
                        ]
                        for j, tile in enumerate(swap_blocks(tiles)):
                            zz[c * 2 + h, pl.ds(jb * 128 + k * 8 + vh * 4 + j, 8, stride=16), :] = tile

    def contracted(c):
        return split(jnp.concatenate([zz[c * 2], zz[c * 2 + 1]], axis=1))

    third = product(weight(1, 0), weight(1, 1), contracted(0), contracted(1))
    for c in range(2):
        for k in range(2):
            for h in range(2):
                for i in range(16):
                    back[pl.ds(i * 64 + h * 4 + k * 2 + c, 8, stride=8), :] = third[c][
                        k * 128 + i * 8 : k * 128 + i * 8 + 8, h * 128 : h * 128 + 128
                    ]

    there = (z * 4 + x) * 4 + y

    def send_back(zt, yt, xt):
        pltpu.make_async_remote_copy(
            back.at[rows(((yt * 8 + zt) * 4 + xt) * 8)],
            home.at[rows(there * 8)],
            back_send,
            back_recv,
            device_id=device(zt, yt, xt, core),
            device_id_type=MESH,
        ).start()

    for i in range(16):
        for dz in (4, 3, 5, 2, 6, 1, 7):
            send_back(at_z(dz), at_y(i & 3), at_x(i >> 2))
        if i:
            send_back(z, at_y(i & 3), at_x(i >> 2))

    home[rows(there * 8), :] = back[rows(((y * 8 + z) * 4 + x) * 8), :]
    part = rows(0, 127 * 8)
    pltpu.make_async_copy(home.at[part], home.at[part], back_recv).wait()

    for i in range(16):
        for h in range(2):
            group = h * 16 + i
            tiles = [home[rows((group * 4 + j) * 8), :] for j in range(4)]
            for j, tile in enumerate(swap_blocks(tiles)):
                for gh in range(2):
                    final[pl.ds(i * 16 + (gh * 4 + j) * 2 + h, 4, stride=256), :] = tile[gh * 4 : gh * 4 + 4]

    def out_here(c):
        return pltpu.make_async_copy(
            final.at[rows(core * 512 + c * 256, 256)], out.at[rows(c * 512 + core * 256, 256)], local_sem.at[c]
        )

    def out_across(c):
        return pltpu.make_async_remote_copy(
            final.at[rows(other * 512 + c * 256, 256)],
            out.at[rows(c * 512 + core * 256, 256)],
            out_send.at[c],
            out_recv.at[c],
            device_id=sibling,
            device_id_type=MESH,
        )

    for c in range(2):
        out_across(c).start()
        out_here(c).start()

    part = rows(0, 127 * 8)
    half_a, half_b = rows(core * 1024, 1024), rows(core * 512, 512)
    pltpu.make_async_copy(ga.at[half_a], ga.at[half_a], core_send.at[0]).wait()
    pltpu.make_async_copy(gb.at[half_b], gb.at[half_b], core_send.at[1]).wait()
    pltpu.make_async_copy(ga.at[rows(0, 56)], ga.at[rows(0, 56)], z_send.at[0]).wait()

    @pl.when(gathers_tail)
    def _():
        pltpu.make_async_copy(gb.at[rows(0, 56)], gb.at[rows(0, 56)], z_send.at[1]).wait()

    for one in rings:
        one[2]()
    pltpu.make_async_copy(sent.at[part], sent.at[part], go_send).wait()
    pltpu.make_async_copy(back.at[part], back.at[part], back_send).wait()
    for c in range(2):
        out_here(c).wait()
        out_across(c).wait()


def hand_over(source, out, held, in_sem, out_sem):
    size = source.shape[0] // in_sem.shape[0]
    parts = [rows(i * size, size) for i in range(in_sem.shape[0])]
    fetches = [pltpu.make_async_copy(source.at[p], held.at[p], in_sem.at[i]) for i, p in enumerate(parts)]
    stores = [pltpu.make_async_copy(held.at[p], out.at[p], out_sem.at[i]) for i, p in enumerate(parts)]
    for fetch in fetches:
        fetch.start()
    for fetch, store in zip(fetches, stores):
        fetch.wait()
        store.start()
    for store in stores:
        store.wait()


def on_device(stem, branch_pair, branch_last):
    dma = pltpu.SemaphoreType.DMA
    whole = pltpu.VMEM((1024, 128), F32)
    result = pl.pallas_call(
        kernel,
        out_shape=jax.ShapeDtypeStruct((1024, 128), F32),
        in_specs=[
            pl.BlockSpec(memory_space=pltpu.HBM),
            pl.BlockSpec(memory_space=pltpu.HBM),
            pl.BlockSpec(memory_space=pltpu.HBM),
        ],
        out_specs=pl.BlockSpec(memory_space=pl.ANY),
        scratch_shapes=[
            whole,
            whole,
            whole,
            pltpu.VMEM((2, 32, 256), F32),
            pltpu.VMEM((2048, 128), F32),
            whole,
            pltpu.VMEM((3, 2, 256, 256), BF16),
            pltpu.VMEM((3, 2, 256, 256), BF16),
            pltpu.VMEM((2, 256, 256), F32),
            pltpu.VMEM((2, 256, 256), F32),
            pltpu.VMEM((4, 256, 128), F32),
            whole,
            whole,
            whole,
            pltpu.SemaphoreType.REGULAR,
            dma((2,)),
            dma((2,)),
            dma((2,)),
            dma((2,)),
            dma((2,)),
            dma((2,)),
            dma((8, 3)),
            dma((8, 3)),
            dma((2,)),
            dma((2,)),
            dma,
            dma,
            dma,
            dma,
            dma((2,)),
            dma((2,)),
        ],
        compiler_params=pltpu.CompilerParams(collective_id=0, has_side_effects=True, vmem_limit_bytes=62 << 20),
        name="absorb",
    )(stem.reshape(1024, 128), branch_pair.reshape(8, 128), branch_last)
    result = pl.pallas_call(
        hand_over,
        out_shape=jax.ShapeDtypeStruct((1024, 128), F32),
        in_specs=[pl.BlockSpec(memory_space=pltpu.HBM)],
        out_specs=pl.BlockSpec(memory_space=pltpu.HBM),
        scratch_shapes=[whole, dma((4,)), dma((4,))],
        compiler_params=pltpu.CompilerParams(vmem_limit_bytes=62 << 20),
        name="hand_over",
    )(result)
    return result.reshape(stem.shape)


def solution(mesh):
    in_specs = (
        P(None, None, "wide", None, "narrow", None),
        P(None, None, ("wide", "narrow"), None),
        P(None, "narrow", None),
    )
    out_specs = P(None, None, "wide", None, "narrow", None)
    return jax.shard_map(on_device, mesh=mesh, in_specs=in_specs, out_specs=out_specs, check_vma=False)
```

```python
import functools

import jax
import jax.numpy as jnp
from jax import lax
from jax.experimental import pallas as pl
from jax.experimental.pallas import tpu as pltpu
from jax.sharding import PartitionSpec as P

MESH = pl.DeviceIdType.MESH
F32 = jnp.float32
BF16 = jnp.bfloat16
ORDER = ("h", "tp", "z", "r0", "p", "t0", "r1", "r2", "t1", "t2", "t3", "r3", "g", "c")


def rows(start, count=8):
    return pl.ds(start if isinstance(start, int) else pl.multiple_of(start, 8), count)


def device(z, y, x, core):
    return ((z & 3) * 8 + x * 2 + core, (z >> 2) * 4 + y)


def swap_blocks(tiles):
    lane = lax.broadcasted_iota(jnp.int32, tiles[0].shape, 1)
    low64 = lane < 64
    low32 = (lane & 32) == 0

    def halves(a, b):
        r = pltpu.roll(jnp.where(low64, b, a), 64, 1)
        return jnp.where(low64, a, r), jnp.where(low64, r, b)

    def quarters(a, b):
        return (
            jnp.where(low32, a, pltpu.roll(b, 32, 1)),
            jnp.where(low32, pltpu.roll(a, 96, 1), b),
        )

    a0, a2 = halves(tiles[0], tiles[2])
    a1, a3 = halves(tiles[1], tiles[3])
    return (*quarters(a0, a1), *quarters(a2, a3))


def split(values):
    high = values.astype(BF16)
    return high, (values - high.astype(F32)).astype(BF16)


def dot(a, b):
    return jnp.dot(a, b, preferred_element_type=F32)


def product(ar, ai, br, bi):
    def left(v):
        return jnp.concatenate([v[0], v[0], v[1]], axis=1)

    def right(v):
        return jnp.concatenate([v[0], v[1], v[0]], axis=0)

    lr, li, rr, ri = left(ar), left(ai), right(br), right(bi)
    return dot(lr, rr) - dot(li, ri), dot(lr, ri) + dot(li, rr)


def kernel(
    stem,
    pair,
    tail,
    out,
    xr,
    sent,
    got,
    tails,
    ga,
    gb,
    wh,
    wl,
    x1,
    y2,
    zz,
    back,
    home,
    final,
    plane_sem,
    local_sem,
    branch_sem,
    pair_send,
    pair_recv,
    z_send,
    z_recv,
    ring_send,
    ring_recv,
    core_send,
    core_recv,
    go_send,
    go_recv,
    back_send,
    back_recv,
    here_sem,
    out_send,
    out_recv,
):
    wide, narrow = lax.axis_index("wide"), lax.axis_index("narrow")
    core, x = wide & 1, (wide >> 1) & 3
    z, y = (narrow >> 2) * 4 + (wide >> 3), narrow & 3
    other = 1 - core
    sibling = device(z, y, x, other)

    def at_z(d):
        return (z + d) & 7

    def at_x(d):
        return (x + d) & 3

    def at_y(d):
        return (y + d) & 3

    def own_half(c):
        return pltpu.make_async_copy(
            stem.at[rows(c * 512 + core * 256, 256)],
            xr.at[rows(core * 512 + c * 256, 256)],
            local_sem.at[c],
        )

    barrier = pltpu.get_barrier_semaphore()
    for d in (4, 3, 5, 2, 6, 1, 7):
        pl.semaphore_signal(barrier, inc=1, device_id=device(at_z(d), y, x, core), device_id_type=MESH)
    for d in range(1, 16):
        pl.semaphore_signal(
            barrier, inc=1, device_id=device(z, at_y(d // 4), at_x(d % 4), core), device_id_type=MESH
        )
    pl.semaphore_signal(barrier, inc=1, device_id=sibling, device_id_type=MESH)

    slot_a = ((core * 4 + y) * 8 + z) * 4 + x
    slot_b = (z * 4 + x) * 4 + y
    fetches = [
        pltpu.make_async_copy(tail, tails, branch_sem.at[0]),
        pltpu.make_async_copy(pair, ga.at[rows(slot_a * 8)], branch_sem.at[1]),
    ]
    for fetch in fetches:
        fetch.start()
    for c in range(2):
        own_half(c).start()

    for fetch in fetches:
        fetch.wait()
    gathers_tail = (z >> 2) == core

    @pl.when(gathers_tail)
    def _():
        line = lax.broadcasted_iota(jnp.int32, (8, 128), 0)
        pieces = []
        for f in range(2):
            for c in range(2):
                for h in range(2):
                    tile = tails[c, rows(f * 16 + ((z >> 1) & 1) * 8), h * 128 : h * 128 + 128]
                    tile = jnp.where(line == (z & 1) * 4 + x, tile, 0.0)
                    pieces.append(jnp.sum(tile, axis=0, keepdims=True))
        gb[rows(slot_b * 8), :] = jnp.concatenate(pieces, axis=0)

    pl.semaphore_wait(barrier, 23)

    for d in range(1, 8):
        pl.semaphore_signal(plane_sem, inc=1, device_id=device(at_z(d), y, x, core), device_id_type=MESH)

    def half_across(c):
        return pltpu.make_async_remote_copy(
            stem.at[rows(c * 512 + other * 256, 256)],
            xr.at[rows(core * 512 + c * 256, 256)],
            pair_send.at[c],
            pair_recv.at[c],
            device_id=sibling,
            device_id_type=MESH,
        )

    for c in range(2):
        half_across(c).start()

    def along_z(buffer, which, slot, d):
        return pltpu.make_async_remote_copy(
            buffer.at[rows(slot * 8)],
            buffer.at[rows(slot * 8)],
            z_send.at[which],
            z_recv.at[which],
            device_id=device(at_z(d), y, x, core),
            device_id_type=MESH,
        )

    for d in (4, 3, 5, 2, 6, 1, 7):
        along_z(ga, 0, slot_a, d).start()

    @pl.when(gathers_tail)
    def _():
        for d in (4, 3, 5, 2, 6, 1, 7):
            along_z(gb, 1, slot_b, d).start()

    pairs = ga.reshape(2, 4, 2, 4, 4, 8, 128)
    rests = gb.reshape(2, 2, 2, 4, 4, 8, 128)

    def on_x(d):
        return at_x(d), device(z, y, at_x(d), core)

    def on_y(d):
        return at_y(d), device(z, at_y(d), x, core)

    def across(which, ref):
        return pltpu.make_async_remote_copy(
            ref, ref, core_send.at[which], core_recv.at[which], device_id=sibling, device_id_type=MESH
        )

    def ring(number, block, place, which=None):
        def copy(d, holder):
            ref = block(place(holder)[0])
            return pltpu.make_async_remote_copy(
                ref,
                ref,
                ring_send.at[number, d - 1],
                ring_recv.at[number, d - 1],
                device_id=place(d)[1],
                device_id_type=MESH,
            )

        def pass_on(holder):
            if which is not None:
                across(which, block(place(holder)[0])).start()

        def start():
            for d in (2, 1, 3):
                copy(d, 0).start()
            pass_on(0)

        def arrive():
            for d in (1, 3, 2):
                copy(d, -d).wait_recv()
                pass_on(-d)

        def drain():
            for d in (1, 2, 3):
                copy(d, 0).wait_send()

        return start, arrive, drain

    rings = [
        ring(0, lambda p: pairs.at[core, y, 0, :, p], on_x),
        ring(1, lambda p: pairs.at[core, p, 1, :, x], on_y),
        ring(2, lambda p: rests.at[core, 0, :, p, y], on_x),
        ring(3, lambda p: rests.at[core, 1, :, x, p], on_y),
        ring(4, lambda p: pairs.at[core, p, 0], on_y, 0),
        ring(5, lambda p: pairs.at[core, :, 1, :, p], on_x, 0),
        ring(6, lambda p: rests.at[core, 0, :, :, p], on_y, 1),
        ring(7, lambda p: rests.at[core, 1, :, p], on_x, 1),
    ]

    here = (((z & 3) * 4 + x) * 2 + (z >> 2)) * 4 + y

    def shuffle_group(number, zt, xt):
        base = ((zt & 3) * 4 + xt) * 16 + (zt >> 2)
        tiles = [xr[pl.ds(i * 256 + base, 8, stride=2), :] for i in range(4)]
        for j, tile in enumerate(swap_blocks(tiles)):
            sent[rows((number * 4 + j) * 8), :] = tile

    def send_tile(number, zt, yt, xt):
        pltpu.make_async_remote_copy(
            sent.at[rows((number * 4 + yt) * 8)],
            got.at[rows(here * 8)],
            go_send,
            go_recv,
            device_id=device(zt, yt, xt, core),
            device_id_type=MESH,
        ).start()

    def send_groups(dx, dzs):
        for dz in dzs:
            zt, xt = at_z(dz), at_x(dx)
            number = dx * 8 + dz
            shuffle_group(number, zt, xt)
            for dy in range(4):
                send_tile(number, zt, at_y(dy), xt)

    def wait_z():
        part = rows(0, 56)
        pltpu.make_async_copy(ga.at[part], ga.at[part], z_recv.at[0]).wait()

        def wait_tail(count):
            part = rows(0, count * 8)
            pltpu.make_async_copy(gb.at[part], gb.at[part], z_recv.at[1]).wait()

        @pl.when(gathers_tail)
        def _():
            wait_tail(3)

        @pl.when(jnp.logical_not(gathers_tail))
        def _():
            wait_tail(4)

    def wait_halves():
        for c in range(2):
            own_half(c).wait()
        for c in range(2):
            half_across(c).wait()

    def wait_planes():
        pl.semaphore_wait(plane_sem, 7)

    def both(first, step):
        for one in rings[first : first + 4]:
            one[step]()

    def tiles_to(dx):
        send_groups(dx, (4, 3, 5, 2, 6, 1, 7))

    def tiles_plane():
        send_groups(1, (0,))
        send_groups(2, (0,))
        send_groups(3, (0,))
        shuffle_group(0, z, x)
        for dy in range(1, 4):
            send_tile(0, z, at_y(dy), x)
        got[rows(here * 8), :] = sent[rows(y * 8), :]

    def wait_across():
        half_a, half_b = rows(other * 1024, 1024), rows(other * 512, 512)
        pltpu.make_async_copy(ga.at[half_a], ga.at[half_a], core_recv.at[0]).wait()
        pltpu.make_async_copy(gb.at[half_b], gb.at[half_b], core_recv.at[1]).wait()

    def arrived():
        part = rows(0, 127 * 8)
        pltpu.make_async_copy(got.at[part], got.at[part], go_recv).wait()

        for i in range(16):
            for h in range(2):
                tiles = [got[rows((i * 8 + h * 4 + j) * 8), :] for j in range(4)]
                for k, tile in enumerate(swap_blocks(tiles)):
                    x1[k % 2, rows(i * 16 + (k // 2) * 8), h * 128 : h * 128 + 128] = tile

    steps = dict(
        g=arrived,
        z=wait_z,
        h=wait_halves,
        p=wait_planes,
        tp=tiles_plane,
        t0=functools.partial(tiles_to, 0),
        t1=functools.partial(tiles_to, 1),
        t2=functools.partial(tiles_to, 2),
        t3=functools.partial(tiles_to, 3),
        r0=functools.partial(both, 0, 0),
        r1=functools.partial(both, 0, 1),
        r2=functools.partial(both, 4, 0),
        r3=functools.partial(both, 4, 1),
        c=wait_across,
    )
    for step in ORDER:
        steps[step]()

    def weights(step, c):
        halves = []
        for h in range(2):
            k = step * 4 + c * 2 + h
            halves.append(jnp.concatenate([ga[pl.ds(i * 64 + k, 8, stride=8), :] for i in range(32)], axis=0))
        return jnp.concatenate(halves, axis=1)

    def tail_weights(c):
        halves = []
        for h in range(2):
            blocks = []
            for n in range(8):
                for f in range(2):
                    for j in range(2):
                        start = ((n // 4) * 64 + j * 32 + n % 4) * 8 + f * 4 + c * 2 + h
                        blocks.append(gb[pl.ds(start, 8, stride=32), :])
            halves.append(jnp.concatenate(blocks, axis=0))
        return jnp.concatenate(halves, axis=1)

    for c in range(2):
        for step in range(2):
            wh[step, c], wl[step, c] = split(weights(step, c))
        wh[2, c], wl[2, c] = split(tail_weights(c).T)

    def weight(number, c):
        return wh[number, c], wl[number, c]

    first = product(weight(0, 0), weight(0, 1), split(x1[0]), split(x1[1]))
    second = product(split(first[0]), split(first[1]), weight(2, 0), weight(2, 1))
    y2[0] = second[0]
    y2[1] = second[1]
    for c in range(2):
        for k in range(2):
            for h in range(2):
                for vh in range(2):
                    for jb in range(2):
                        tiles = [
                            y2[c, rows(k * 128 + j * 32 + h * 16 + jb * 8), vh * 128 : vh * 128 + 128] for j in range(4)
                        ]
                        for j, tile in enumerate(swap_blocks(tiles)):
                            zz[c * 2 + h, pl.ds(jb * 128 + k * 8 + vh * 4 + j, 8, stride=16), :] = tile

    def contracted(c):
        return split(jnp.concatenate([zz[c * 2], zz[c * 2 + 1]], axis=1))

    third = product(weight(1, 0), weight(1, 1), contracted(0), contracted(1))
    for c in range(2):
        for k in range(2):
            for h in range(2):
                for i in range(16):
                    back[pl.ds(i * 64 + h * 4 + k * 2 + c, 8, stride=8), :] = third[c][
                        k * 128 + i * 8 : k * 128 + i * 8 + 8, h * 128 : h * 128 + 128
                    ]

    there = (z * 4 + x) * 4 + y

    def send_back(dz, yt, xt):
        zt = at_z(dz)
        pltpu.make_async_remote_copy(
            back.at[rows(((yt * 8 + zt) * 4 + xt) * 8)],
            home.at[rows(there * 8)],
            back_send,
            back_recv.at[dz & 3],
            device_id=device(zt, yt, xt, core),
            device_id_type=MESH,
        ).start()

    for dzs in ((4, 2, 6, 0), (5, 3, 1, 7)):
        for i in range(16):
            for dz in dzs:
                if i or dz:
                    send_back(dz, at_y(i & 3), at_x(i >> 2))

    def out_here(zl, j, c):
        return pltpu.make_async_copy(
            final.at[rows(core * 512 + c * 256 + zl * 64, 64)],
            out.at[rows(c * 512 + core * 256 + zl * 64, 64)],
            here_sem.at[j, c],
        )

    def out_across(zl, j, c):
        return pltpu.make_async_remote_copy(
            final.at[rows(other * 512 + c * 256 + zl * 64, 64)],
            out.at[rows(c * 512 + core * 256 + zl * 64, 64)],
            out_send.at[j, c],
            out_recv.at[j, c],
            device_id=sibling,
            device_id_type=MESH,
        )

    home[rows(there * 8), :] = back[rows(((y * 8 + z) * 4 + x) * 8), :]
    for j in (0, 2, 1, 3):
        part = rows(0, (32 if j else 31) * 8)
        pltpu.make_async_copy(home.at[part], home.at[part], back_recv.at[j]).wait()
        zl = (z - j) & 3
        for i in range(4):
            for h in range(2):
                group = (h * 4 + zl) * 4 + i
                tiles = [home[rows((group * 4 + k) * 8), :] for k in range(4)]
                for k, tile in enumerate(swap_blocks(tiles)):
                    for gh in range(2):
                        line = (zl * 4 + i) * 16 + (gh * 4 + k) * 2 + h
                        final[pl.ds(line, 4, stride=256), :] = tile[gh * 4 : gh * 4 + 4]
        for c in range(2):
            out_across(zl, j, c).start()
            out_here(zl, j, c).start()

    part = rows(0, 127 * 8)
    half_a, half_b = rows(core * 1024, 1024), rows(core * 512, 512)
    pltpu.make_async_copy(ga.at[half_a], ga.at[half_a], core_send.at[0]).wait()
    pltpu.make_async_copy(gb.at[half_b], gb.at[half_b], core_send.at[1]).wait()
    pltpu.make_async_copy(ga.at[rows(0, 56)], ga.at[rows(0, 56)], z_send.at[0]).wait()

    @pl.when(gathers_tail)
    def _():
        pltpu.make_async_copy(gb.at[rows(0, 56)], gb.at[rows(0, 56)], z_send.at[1]).wait()

    for one in rings:
        one[2]()
    pltpu.make_async_copy(sent.at[part], sent.at[part], go_send).wait()
    pltpu.make_async_copy(back.at[part], back.at[part], back_send).wait()
    for j in range(4):
        for c in range(2):
            out_here((z - j) & 3, j, c).wait()
            out_across((z - j) & 3, j, c).wait()


def hand_over(source, out, held, in_sem, out_sem):
    size = source.shape[0] // in_sem.shape[0]
    parts = [rows(i * size, size) for i in range(in_sem.shape[0])]
    fetches = [pltpu.make_async_copy(source.at[p], held.at[p], in_sem.at[i]) for i, p in enumerate(parts)]
    stores = [pltpu.make_async_copy(held.at[p], out.at[p], out_sem.at[i]) for i, p in enumerate(parts)]
    for fetch in fetches:
        fetch.start()
    for fetch, store in zip(fetches, stores):
        fetch.wait()
        store.start()
    for store in stores:
        store.wait()


def on_device(stem, branch_pair, branch_last):
    dma = pltpu.SemaphoreType.DMA
    whole = pltpu.VMEM((1024, 128), F32)
    result = pl.pallas_call(
        kernel,
        out_shape=jax.ShapeDtypeStruct((1024, 128), F32),
        in_specs=[
            pl.BlockSpec(memory_space=pltpu.HBM),
            pl.BlockSpec(memory_space=pltpu.HBM),
            pl.BlockSpec(memory_space=pltpu.HBM),
        ],
        out_specs=pl.BlockSpec(memory_space=pl.ANY),
        scratch_shapes=[
            whole,
            whole,
            whole,
            pltpu.VMEM((2, 32, 256), F32),
            pltpu.VMEM((2048, 128), F32),
            whole,
            pltpu.VMEM((3, 2, 256, 256), BF16),
            pltpu.VMEM((3, 2, 256, 256), BF16),
            pltpu.VMEM((2, 256, 256), F32),
            pltpu.VMEM((2, 256, 256), F32),
            pltpu.VMEM((4, 256, 128), F32),
            whole,
            whole,
            whole,
            pltpu.SemaphoreType.REGULAR,
            dma((2,)),
            dma((2,)),
            dma((2,)),
            dma((2,)),
            dma((2,)),
            dma((2,)),
            dma((8, 3)),
            dma((8, 3)),
            dma((2,)),
            dma((2,)),
            dma,
            dma,
            dma,
            dma((4,)),
            dma((4, 2)),
            dma((4, 2)),
            dma((4, 2)),
        ],
        compiler_params=pltpu.CompilerParams(collective_id=0, has_side_effects=True, vmem_limit_bytes=62 << 20),
        name="absorb",
    )(stem.reshape(1024, 128), branch_pair.reshape(8, 128), branch_last)
    result = pl.pallas_call(
        hand_over,
        out_shape=jax.ShapeDtypeStruct((1024, 128), F32),
        in_specs=[pl.BlockSpec(memory_space=pltpu.HBM)],
        out_specs=pl.BlockSpec(memory_space=pltpu.HBM),
        scratch_shapes=[whole, dma((4,)), dma((4,))],
        compiler_params=pltpu.CompilerParams(vmem_limit_bytes=62 << 20),
        name="hand_over",
    )(result)
    return result.reshape(stem.shape)


def solution(mesh):
    in_specs = (
        P(None, None, "wide", None, "narrow", None),
        P(None, None, ("wide", "narrow"), None),
        P(None, "narrow", None),
    )
    out_specs = P(None, None, "wide", None, "narrow", None)
    return jax.shard_map(on_device, mesh=mesh, in_specs=in_specs, out_specs=out_specs, check_vma=False)
```

```python
import functools

import jax
import jax.numpy as jnp
from jax import lax
from jax.experimental import pallas as pl
from jax.experimental.pallas import tpu as pltpu
from jax.sharding import PartitionSpec as P

MESH = pl.DeviceIdType.MESH
F32 = jnp.float32
BF16 = jnp.bfloat16
ORDER = ("h", "tp", "z", "r0", "p", "t0", "r1", "r2", "t1", "t2", "t3", "r3", "g", "c")


def rows(start, count=8):
    return pl.ds(start if isinstance(start, int) else pl.multiple_of(start, 8), count)


def device(z, y, x, core):
    return ((z & 3) * 8 + x * 2 + core, (z >> 2) * 4 + y)


def swap_blocks(tiles):
    lane = lax.broadcasted_iota(jnp.int32, tiles[0].shape, 1)
    low64 = lane < 64
    low32 = (lane & 32) == 0

    def halves(a, b):
        r = pltpu.roll(jnp.where(low64, b, a), 64, 1)
        return jnp.where(low64, a, r), jnp.where(low64, r, b)

    def quarters(a, b):
        return (
            jnp.where(low32, a, pltpu.roll(b, 32, 1)),
            jnp.where(low32, pltpu.roll(a, 96, 1), b),
        )

    a0, a2 = halves(tiles[0], tiles[2])
    a1, a3 = halves(tiles[1], tiles[3])
    return (*quarters(a0, a1), *quarters(a2, a3))


def split(values):
    high = values.astype(BF16)
    return high, (values - high.astype(F32)).astype(BF16)


def dot(a, b):
    return jnp.dot(a, b, preferred_element_type=F32)


def product(ar, ai, br, bi):
    def left(v):
        return jnp.concatenate([v[0], v[0], v[1]], axis=1)

    def right(v):
        return jnp.concatenate([v[0], v[1], v[0]], axis=0)

    lr, li, rr, ri = left(ar), left(ai), right(br), right(bi)
    return dot(lr, rr) - dot(li, ri), dot(lr, ri) + dot(li, rr)


def kernel(
    stem,
    pair,
    tail,
    out,
    xr,
    sent,
    got,
    tails,
    ga,
    gb,
    wh,
    wl,
    x1,
    y2,
    zz,
    back,
    home,
    final,
    plane_sem,
    local_sem,
    branch_sem,
    pair_send,
    pair_recv,
    z_send,
    z_recv,
    ring_send,
    ring_recv,
    core_send,
    core_recv,
    go_send,
    go_recv,
    back_send,
    back_recv,
    here_sem,
    own_sem,
):
    wide, narrow = lax.axis_index("wide"), lax.axis_index("narrow")
    core, x = wide & 1, (wide >> 1) & 3
    z, y = (narrow >> 2) * 4 + (wide >> 3), narrow & 3
    other = 1 - core
    sibling = device(z, y, x, other)

    def at_z(d):
        return (z + d) & 7

    def at_x(d):
        return (x + d) & 3

    def at_y(d):
        return (y + d) & 3

    def own_half(c):
        return pltpu.make_async_copy(
            stem.at[rows(c * 512 + core * 256, 256)],
            xr.at[rows(core * 512 + c * 256, 256)],
            local_sem.at[c],
        )

    barrier = pltpu.get_barrier_semaphore()
    for d in (4, 3, 5, 2, 6, 1, 7):
        pl.semaphore_signal(barrier, inc=1, device_id=device(at_z(d), y, x, core), device_id_type=MESH)
    for d in range(1, 16):
        pl.semaphore_signal(
            barrier, inc=1, device_id=device(z, at_y(d // 4), at_x(d % 4), core), device_id_type=MESH
        )
    pl.semaphore_signal(barrier, inc=1, device_id=sibling, device_id_type=MESH)

    slot_a = ((core * 4 + y) * 8 + z) * 4 + x
    slot_b = (z * 4 + x) * 4 + y
    fetches = [
        pltpu.make_async_copy(tail, tails, branch_sem.at[0]),
        pltpu.make_async_copy(pair, ga.at[rows(slot_a * 8)], branch_sem.at[1]),
    ]
    for fetch in fetches:
        fetch.start()
    for c in range(2):
        own_half(c).start()

    for fetch in fetches:
        fetch.wait()
    gathers_tail = (z >> 2) == core

    @pl.when(gathers_tail)
    def _():
        line = lax.broadcasted_iota(jnp.int32, (8, 128), 0)
        pieces = []
        for f in range(2):
            for c in range(2):
                for h in range(2):
                    tile = tails[c, rows(f * 16 + ((z >> 1) & 1) * 8), h * 128 : h * 128 + 128]
                    tile = jnp.where(line == (z & 1) * 4 + x, tile, 0.0)
                    pieces.append(jnp.sum(tile, axis=0, keepdims=True))
        gb[rows(slot_b * 8), :] = jnp.concatenate(pieces, axis=0)

    pl.semaphore_wait(barrier, 23)

    for d in range(1, 8):
        pl.semaphore_signal(plane_sem, inc=1, device_id=device(at_z(d), y, x, core), device_id_type=MESH)

    def half_across(c):
        return pltpu.make_async_remote_copy(
            stem.at[rows(c * 512 + other * 256, 256)],
            xr.at[rows(core * 512 + c * 256, 256)],
            pair_send.at[c],
            pair_recv.at[c],
            device_id=sibling,
            device_id_type=MESH,
        )

    for c in range(2):
        half_across(c).start()

    def along_z(buffer, which, slot, d):
        return pltpu.make_async_remote_copy(
            buffer.at[rows(slot * 8)],
            buffer.at[rows(slot * 8)],
            z_send.at[which],
            z_recv.at[which],
            device_id=device(at_z(d), y, x, core),
            device_id_type=MESH,
        )

    for d in (4, 3, 5, 2, 6, 1, 7):
        along_z(ga, 0, slot_a, d).start()

    @pl.when(gathers_tail)
    def _():
        for d in (4, 3, 5, 2, 6, 1, 7):
            along_z(gb, 1, slot_b, d).start()

    pairs = ga.reshape(2, 4, 2, 4, 4, 8, 128)
    rests = gb.reshape(2, 2, 2, 4, 4, 8, 128)

    def on_x(d):
        return at_x(d), device(z, y, at_x(d), core)

    def on_y(d):
        return at_y(d), device(z, at_y(d), x, core)

    def across(which, ref):
        return pltpu.make_async_remote_copy(
            ref, ref, core_send.at[which], core_recv.at[which], device_id=sibling, device_id_type=MESH
        )

    def ring(number, block, place, which=None):
        def copy(d, holder):
            ref = block(place(holder)[0])
            return pltpu.make_async_remote_copy(
                ref,
                ref,
                ring_send.at[number, d - 1],
                ring_recv.at[number, d - 1],
                device_id=place(d)[1],
                device_id_type=MESH,
            )

        def pass_on(holder):
            if which is not None:
                across(which, block(place(holder)[0])).start()

        def start():
            for d in (2, 1, 3):
                copy(d, 0).start()
            pass_on(0)

        def arrive():
            for d in (1, 3, 2):
                copy(d, -d).wait_recv()
                pass_on(-d)

        def drain():
            for d in (1, 2, 3):
                copy(d, 0).wait_send()

        return start, arrive, drain

    rings = [
        ring(0, lambda p: pairs.at[core, y, 0, :, p], on_x),
        ring(1, lambda p: pairs.at[core, p, 1, :, x], on_y),
        ring(2, lambda p: rests.at[core, 0, :, p, y], on_x),
        ring(3, lambda p: rests.at[core, 1, :, x, p], on_y),
        ring(4, lambda p: pairs.at[core, p, 0], on_y, 0),
        ring(5, lambda p: pairs.at[core, :, 1, :, p], on_x, 0),
        ring(6, lambda p: rests.at[core, 0, :, :, p], on_y, 1),
        ring(7, lambda p: rests.at[core, 1, :, p], on_x, 1),
    ]

    here = (((z & 3) * 4 + x) * 2 + (z >> 2)) * 4 + y

    def shuffle_group(number, zt, xt):
        base = ((zt & 3) * 4 + xt) * 16 + (zt >> 2)
        tiles = [xr[pl.ds(i * 256 + base, 8, stride=2), :] for i in range(4)]
        for j, tile in enumerate(swap_blocks(tiles)):
            sent[rows((number * 4 + j) * 8), :] = tile

    def send_tile(number, zt, yt, xt):
        pltpu.make_async_remote_copy(
            sent.at[rows((number * 4 + yt) * 8)],
            got.at[rows(here * 8)],
            go_send,
            go_recv,
            device_id=device(zt, yt, xt, core),
            device_id_type=MESH,
        ).start()

    def send_groups(dx, dzs):
        for dz in dzs:
            zt, xt = at_z(dz), at_x(dx)
            number = dx * 8 + dz
            shuffle_group(number, zt, xt)
            for dy in range(4):
                send_tile(number, zt, at_y(dy), xt)

    def wait_z():
        part = rows(0, 56)
        pltpu.make_async_copy(ga.at[part], ga.at[part], z_recv.at[0]).wait()

        def wait_tail(count):
            part = rows(0, count * 8)
            pltpu.make_async_copy(gb.at[part], gb.at[part], z_recv.at[1]).wait()

        @pl.when(gathers_tail)
        def _():
            wait_tail(3)

        @pl.when(jnp.logical_not(gathers_tail))
        def _():
            wait_tail(4)

    def wait_halves():
        for c in range(2):
            own_half(c).wait()
        for c in range(2):
            half_across(c).wait()

    def wait_planes():
        pl.semaphore_wait(plane_sem, 7)

    def both(first, step):
        for one in rings[first : first + 4]:
            one[step]()

    def tiles_to(dx):
        send_groups(dx, (4, 3, 5, 2, 6, 1, 7))

    def tiles_plane():
        send_groups(1, (0,))
        send_groups(2, (0,))
        send_groups(3, (0,))
        shuffle_group(0, z, x)
        for dy in range(1, 4):
            send_tile(0, z, at_y(dy), x)
        got[rows(here * 8), :] = sent[rows(y * 8), :]

    def wait_across():
        half_a, half_b = rows(other * 1024, 1024), rows(other * 512, 512)
        pltpu.make_async_copy(ga.at[half_a], ga.at[half_a], core_recv.at[0]).wait()
        pltpu.make_async_copy(gb.at[half_b], gb.at[half_b], core_recv.at[1]).wait()

    def arrived():
        part = rows(0, 127 * 8)
        pltpu.make_async_copy(got.at[part], got.at[part], go_recv).wait()

        for i in range(16):
            for h in range(2):
                tiles = [got[rows((i * 8 + h * 4 + j) * 8), :] for j in range(4)]
                for k, tile in enumerate(swap_blocks(tiles)):
                    x1[k % 2, rows(i * 16 + (k // 2) * 8), h * 128 : h * 128 + 128] = tile

    steps = dict(
        g=arrived,
        z=wait_z,
        h=wait_halves,
        p=wait_planes,
        tp=tiles_plane,
        t0=functools.partial(tiles_to, 0),
        t1=functools.partial(tiles_to, 1),
        t2=functools.partial(tiles_to, 2),
        t3=functools.partial(tiles_to, 3),
        r0=functools.partial(both, 0, 0),
        r1=functools.partial(both, 0, 1),
        r2=functools.partial(both, 4, 0),
        r3=functools.partial(both, 4, 1),
        c=wait_across,
    )
    for step in ORDER:
        steps[step]()

    def weights(step, c):
        halves = []
        for h in range(2):
            k = step * 4 + c * 2 + h
            halves.append(jnp.concatenate([ga[pl.ds(i * 64 + k, 8, stride=8), :] for i in range(32)], axis=0))
        return jnp.concatenate(halves, axis=1)

    def tail_weights(c):
        halves = []
        for h in range(2):
            blocks = []
            for n in range(8):
                for f in range(2):
                    for j in range(2):
                        start = ((n // 4) * 64 + j * 32 + n % 4) * 8 + f * 4 + c * 2 + h
                        blocks.append(gb[pl.ds(start, 8, stride=32), :])
            halves.append(jnp.concatenate(blocks, axis=0))
        return jnp.concatenate(halves, axis=1)

    for c in range(2):
        for step in range(2):
            wh[step, c], wl[step, c] = split(weights(step, c))
        wh[2, c], wl[2, c] = split(tail_weights(c).T)

    def weight(number, c):
        return wh[number, c], wl[number, c]

    first = product(weight(0, 0), weight(0, 1), split(x1[0]), split(x1[1]))
    second = product(split(first[0]), split(first[1]), weight(2, 0), weight(2, 1))
    y2[0] = second[0]
    y2[1] = second[1]
    for c in range(2):
        for k in range(2):
            for h in range(2):
                for vh in range(2):
                    for jb in range(2):
                        tiles = [
                            y2[c, rows(k * 128 + j * 32 + h * 16 + jb * 8), vh * 128 : vh * 128 + 128] for j in range(4)
                        ]
                        for j, tile in enumerate(swap_blocks(tiles)):
                            zz[c * 2 + h, pl.ds(jb * 128 + k * 8 + vh * 4 + j, 8, stride=16), :] = tile

    def contracted(c):
        return split(jnp.concatenate([zz[c * 2], zz[c * 2 + 1]], axis=1))

    third = product(weight(1, 0), weight(1, 1), contracted(0), contracted(1))
    for c in range(2):
        for k in range(2):
            for h in range(2):
                for i in range(16):
                    back[pl.ds(i * 64 + k * 4 + h * 2 + c, 8, stride=8), :] = third[c][
                        k * 128 + i * 8 : k * 128 + i * 8 + 8, h * 128 : h * 128 + 128
                    ]

    there = (z * 4 + x) * 4 + y

    def half(tile, which):
        return pl.ds(pl.multiple_of(tile * 8 + which * 4, 4), 4)

    def send_back(dz, yt, xt, to_core):
        zt = at_z(dz)
        pltpu.make_async_remote_copy(
            back.at[half((yt * 8 + zt) * 4 + xt, to_core)],
            home.at[half(there, core)],
            back_send,
            back_recv.at[dz & 3],
            device_id=device(zt, yt, xt, to_core),
            device_id_type=MESH,
        ).start()

    for dzs in ((4, 2, 6, 0), (5, 3, 1, 7)):
        for i in range(16):
            for dz in dzs:
                for to_core in (core, other):
                    if i or dz or to_core is other:
                        send_back(dz, at_y(i & 3), at_x(i >> 2), to_core)
    own = pltpu.make_async_copy(
        back.at[half((y * 8 + z) * 4 + x, core)], home.at[half(there, core)], own_sem
    )
    own.start()
    own.wait()

    parts = out.reshape(2, 2, 4, 4, 2, 8, 128)
    for j in (0, 2, 1, 3):
        part = rows(0, 256) if j else pl.ds(0, 252)
        pltpu.make_async_copy(home.at[part], home.at[part], back_recv.at[j]).wait()
        zl = (z - j) & 3
        for i in range(4):
            for h in range(2):
                group = (h * 4 + zl) * 4 + i
                tiles = [home[rows((group * 4 + k) * 8), :] for k in range(4)]
                for k, tile in enumerate(swap_blocks(tiles)):
                    final[pl.ds((zl * 4 + i) * 8 + k * 2 + h, 8, stride=128), :] = tile
        for k in range(8):
            pltpu.make_async_copy(
                final.reshape(8, 4, 4, 8, 128).at[k, zl],
                parts.at[k % 2, k // 4, zl, :, (k // 2) % 2],
                here_sem,
            ).start()

    part = rows(0, 127 * 8)
    half_a, half_b = rows(core * 1024, 1024), rows(core * 512, 512)
    pltpu.make_async_copy(ga.at[half_a], ga.at[half_a], core_send.at[0]).wait()
    pltpu.make_async_copy(gb.at[half_b], gb.at[half_b], core_send.at[1]).wait()
    pltpu.make_async_copy(ga.at[rows(0, 56)], ga.at[rows(0, 56)], z_send.at[0]).wait()

    @pl.when(gathers_tail)
    def _():
        pltpu.make_async_copy(gb.at[rows(0, 56)], gb.at[rows(0, 56)], z_send.at[1]).wait()

    for one in rings:
        one[2]()
    pltpu.make_async_copy(sent.at[part], sent.at[part], go_send).wait()
    part = pl.ds(0, 1020)
    pltpu.make_async_copy(back.at[part], back.at[part], back_send).wait()
    pltpu.make_async_copy(final, final, here_sem).wait()


def hand_over(source, out, held, in_sem, out_sem):
    size = source.shape[0] // in_sem.shape[0]
    parts = [rows(i * size, size) for i in range(in_sem.shape[0])]
    fetches = [pltpu.make_async_copy(source.at[p], held.at[p], in_sem.at[i]) for i, p in enumerate(parts)]
    stores = [pltpu.make_async_copy(held.at[p], out.at[p], out_sem.at[i]) for i, p in enumerate(parts)]
    for fetch in fetches:
        fetch.start()
    for fetch, store in zip(fetches, stores):
        fetch.wait()
        store.start()
    for store in stores:
        store.wait()


def on_device(stem, branch_pair, branch_last):
    dma = pltpu.SemaphoreType.DMA
    whole = pltpu.VMEM((1024, 128), F32)
    result = pl.pallas_call(
        kernel,
        out_shape=jax.ShapeDtypeStruct((1024, 128), F32),
        in_specs=[
            pl.BlockSpec(memory_space=pltpu.HBM),
            pl.BlockSpec(memory_space=pltpu.HBM),
            pl.BlockSpec(memory_space=pltpu.HBM),
        ],
        out_specs=pl.BlockSpec(memory_space=pl.ANY),
        scratch_shapes=[
            whole,
            whole,
            whole,
            pltpu.VMEM((2, 32, 256), F32),
            pltpu.VMEM((2048, 128), F32),
            whole,
            pltpu.VMEM((3, 2, 256, 256), BF16),
            pltpu.VMEM((3, 2, 256, 256), BF16),
            pltpu.VMEM((2, 256, 256), F32),
            pltpu.VMEM((2, 256, 256), F32),
            pltpu.VMEM((4, 256, 128), F32),
            whole,
            whole,
            whole,
            pltpu.SemaphoreType.REGULAR,
            dma((2,)),
            dma((2,)),
            dma((2,)),
            dma((2,)),
            dma((2,)),
            dma((2,)),
            dma((8, 3)),
            dma((8, 3)),
            dma((2,)),
            dma((2,)),
            dma,
            dma,
            dma,
            dma((4,)),
            dma,
            dma,
        ],
        compiler_params=pltpu.CompilerParams(collective_id=0, has_side_effects=True, vmem_limit_bytes=62 << 20),
        name="absorb",
    )(stem.reshape(1024, 128), branch_pair.reshape(8, 128), branch_last)
    result = pl.pallas_call(
        hand_over,
        out_shape=jax.ShapeDtypeStruct((1024, 128), F32),
        in_specs=[pl.BlockSpec(memory_space=pltpu.HBM)],
        out_specs=pl.BlockSpec(memory_space=pltpu.HBM),
        scratch_shapes=[whole, dma((4,)), dma((4,))],
        compiler_params=pltpu.CompilerParams(vmem_limit_bytes=62 << 20),
        name="hand_over",
    )(result)
    return result.reshape(stem.shape)


def solution(mesh):
    in_specs = (
        P(None, None, "wide", None, "narrow", None),
        P(None, None, ("wide", "narrow"), None),
        P(None, "narrow", None),
    )
    out_specs = P(None, None, "wide", None, "narrow", None)
    return jax.shard_map(on_device, mesh=mesh, in_specs=in_specs, out_specs=out_specs, check_vma=False)
```

```python
import functools

import jax
import jax.numpy as jnp
from jax import lax
from jax.experimental import pallas as pl
from jax.experimental.pallas import tpu as pltpu
from jax.sharding import PartitionSpec as P

MESH = pl.DeviceIdType.MESH
F32 = jnp.float32
BF16 = jnp.bfloat16
ORDER = ("h", "tp", "z", "r0", "p", "t0", "r1", "r2", "t1", "t2", "t3", "r3", "g", "c")


def rows(start, count=8):
    return pl.ds(start if isinstance(start, int) else pl.multiple_of(start, 8), count)


def device(z, y, x, core):
    return ((z & 3) * 8 + x * 2 + core, (z >> 2) * 4 + y)


def swap_blocks(tiles):
    lane = lax.broadcasted_iota(jnp.int32, tiles[0].shape, 1)
    low64 = lane < 64
    low32 = (lane & 32) == 0

    def halves(a, b):
        r = pltpu.roll(jnp.where(low64, b, a), 64, 1)
        return jnp.where(low64, a, r), jnp.where(low64, r, b)

    def quarters(a, b):
        return (
            jnp.where(low32, a, pltpu.roll(b, 32, 1)),
            jnp.where(low32, pltpu.roll(a, 96, 1), b),
        )

    a0, a2 = halves(tiles[0], tiles[2])
    a1, a3 = halves(tiles[1], tiles[3])
    return (*quarters(a0, a1), *quarters(a2, a3))


def split(values):
    high = values.astype(BF16)
    return high, (values - high.astype(F32)).astype(BF16)


def dot(a, b):
    return jnp.dot(a, b, preferred_element_type=F32)


def product(ar, ai, br, bi):
    def left(v):
        return jnp.concatenate([v[0], v[0], v[1]], axis=1)

    def right(v):
        return jnp.concatenate([v[0], v[1], v[0]], axis=0)

    lr, li, rr, ri = left(ar), left(ai), right(br), right(bi)
    return dot(lr, rr) - dot(li, ri), dot(lr, ri) + dot(li, rr)


def kernel(
    stem,
    pair,
    tail,
    out,
    xr,
    sent,
    got,
    tails,
    ga,
    gb,
    wh,
    wl,
    x1,
    y2,
    zz,
    back,
    home,
    plane_sem,
    local_sem,
    branch_sem,
    pair_send,
    pair_recv,
    z_send,
    z_recv,
    ring_send,
    ring_recv,
    core_send,
    core_recv,
    go_send,
    go_recv,
    back_send,
    back_recv,
    own_sem,
):
    wide, narrow = lax.axis_index("wide"), lax.axis_index("narrow")
    core, x = wide & 1, (wide >> 1) & 3
    z, y = (narrow >> 2) * 4 + (wide >> 3), narrow & 3
    other = 1 - core
    sibling = device(z, y, x, other)

    def at_z(d):
        return (z + d) & 7

    def at_x(d):
        return (x + d) & 3

    def at_y(d):
        return (y + d) & 3

    def own_half(c):
        return pltpu.make_async_copy(
            stem.at[rows(c * 512 + core * 256, 256)],
            xr.at[rows(core * 512 + c * 256, 256)],
            local_sem.at[c],
        )

    barrier = pltpu.get_barrier_semaphore()
    for d in (4, 3, 5, 2, 6, 1, 7):
        pl.semaphore_signal(barrier, inc=1, device_id=device(at_z(d), y, x, core), device_id_type=MESH)
    for d in range(1, 16):
        pl.semaphore_signal(
            barrier, inc=1, device_id=device(z, at_y(d // 4), at_x(d % 4), core), device_id_type=MESH
        )
    pl.semaphore_signal(barrier, inc=1, device_id=sibling, device_id_type=MESH)

    slot_a = ((core * 4 + y) * 8 + z) * 4 + x
    slot_b = (z * 4 + x) * 4 + y
    fetches = [
        pltpu.make_async_copy(tail, tails, branch_sem.at[0]),
        pltpu.make_async_copy(pair, ga.at[rows(slot_a * 8)], branch_sem.at[1]),
    ]
    for fetch in fetches:
        fetch.start()
    for c in range(2):
        own_half(c).start()

    for fetch in fetches:
        fetch.wait()
    gathers_tail = (z >> 2) == core

    @pl.when(gathers_tail)
    def _():
        line = lax.broadcasted_iota(jnp.int32, (8, 128), 0)
        pieces = []
        for f in range(2):
            for c in range(2):
                for h in range(2):
                    tile = tails[c, rows(f * 16 + ((z >> 1) & 1) * 8), h * 128 : h * 128 + 128]
                    tile = jnp.where(line == (z & 1) * 4 + x, tile, 0.0)
                    pieces.append(jnp.sum(tile, axis=0, keepdims=True))
        gb[rows(slot_b * 8), :] = jnp.concatenate(pieces, axis=0)

    pl.semaphore_wait(barrier, 23)

    for d in range(1, 8):
        pl.semaphore_signal(plane_sem, inc=1, device_id=device(at_z(d), y, x, core), device_id_type=MESH)

    def half_across(c):
        return pltpu.make_async_remote_copy(
            stem.at[rows(c * 512 + other * 256, 256)],
            xr.at[rows(core * 512 + c * 256, 256)],
            pair_send.at[c],
            pair_recv.at[c],
            device_id=sibling,
            device_id_type=MESH,
        )

    for c in range(2):
        half_across(c).start()

    def along_z(buffer, which, slot, d):
        return pltpu.make_async_remote_copy(
            buffer.at[rows(slot * 8)],
            buffer.at[rows(slot * 8)],
            z_send.at[which],
            z_recv.at[which],
            device_id=device(at_z(d), y, x, core),
            device_id_type=MESH,
        )

    for d in (4, 3, 5, 2, 6, 1, 7):
        along_z(ga, 0, slot_a, d).start()

    @pl.when(gathers_tail)
    def _():
        for d in (4, 3, 5, 2, 6, 1, 7):
            along_z(gb, 1, slot_b, d).start()

    pairs = ga.reshape(2, 4, 2, 4, 4, 8, 128)
    rests = gb.reshape(2, 2, 2, 4, 4, 8, 128)

    def on_x(d):
        return at_x(d), device(z, y, at_x(d), core)

    def on_y(d):
        return at_y(d), device(z, at_y(d), x, core)

    def across(which, ref):
        return pltpu.make_async_remote_copy(
            ref, ref, core_send.at[which], core_recv.at[which], device_id=sibling, device_id_type=MESH
        )

    def ring(number, block, place, which=None):
        def copy(d, holder):
            ref = block(place(holder)[0])
            return pltpu.make_async_remote_copy(
                ref,
                ref,
                ring_send.at[number, d - 1],
                ring_recv.at[number, d - 1],
                device_id=place(d)[1],
                device_id_type=MESH,
            )

        def pass_on(holder):
            if which is not None:
                across(which, block(place(holder)[0])).start()

        def start():
            for d in (2, 1, 3):
                copy(d, 0).start()
            pass_on(0)

        def arrive():
            for d in (1, 3, 2):
                copy(d, -d).wait_recv()
                pass_on(-d)

        def drain():
            for d in (1, 2, 3):
                copy(d, 0).wait_send()

        return start, arrive, drain

    rings = [
        ring(0, lambda p: pairs.at[core, y, 0, :, p], on_x),
        ring(1, lambda p: pairs.at[core, p, 1, :, x], on_y),
        ring(2, lambda p: rests.at[core, 0, :, p, y], on_x),
        ring(3, lambda p: rests.at[core, 1, :, x, p], on_y),
        ring(4, lambda p: pairs.at[core, p, 0], on_y, 0),
        ring(5, lambda p: pairs.at[core, :, 1, :, p], on_x, 0),
        ring(6, lambda p: rests.at[core, 0, :, :, p], on_y, 1),
        ring(7, lambda p: rests.at[core, 1, :, p], on_x, 1),
    ]

    here = (((z & 3) * 4 + x) * 2 + (z >> 2)) * 4 + y

    def shuffle_group(number, zt, xt):
        base = ((zt & 3) * 4 + xt) * 16 + (zt >> 2)
        tiles = [xr[pl.ds(i * 256 + base, 8, stride=2), :] for i in range(4)]
        for j, tile in enumerate(swap_blocks(tiles)):
            sent[rows((number * 4 + j) * 8), :] = tile

    def send_tile(number, zt, yt, xt):
        pltpu.make_async_remote_copy(
            sent.at[rows((number * 4 + yt) * 8)],
            got.at[rows(here * 8)],
            go_send,
            go_recv,
            device_id=device(zt, yt, xt, core),
            device_id_type=MESH,
        ).start()

    def send_groups(dx, dzs):
        for dz in dzs:
            zt, xt = at_z(dz), at_x(dx)
            number = dx * 8 + dz
            shuffle_group(number, zt, xt)
            for dy in range(4):
                send_tile(number, zt, at_y(dy), xt)

    def wait_z():
        part = rows(0, 56)
        pltpu.make_async_copy(ga.at[part], ga.at[part], z_recv.at[0]).wait()

        def wait_tail(count):
            part = rows(0, count * 8)
            pltpu.make_async_copy(gb.at[part], gb.at[part], z_recv.at[1]).wait()

        @pl.when(gathers_tail)
        def _():
            wait_tail(3)

        @pl.when(jnp.logical_not(gathers_tail))
        def _():
            wait_tail(4)

    def wait_halves():
        for c in range(2):
            own_half(c).wait()
        for c in range(2):
            half_across(c).wait()

    def wait_planes():
        pl.semaphore_wait(plane_sem, 7)

    def both(first, step):
        for one in rings[first : first + 4]:
            one[step]()

    def tiles_to(dx):
        send_groups(dx, (4, 3, 5, 2, 6, 1, 7))

    def tiles_plane():
        send_groups(1, (0,))
        send_groups(2, (0,))
        send_groups(3, (0,))
        shuffle_group(0, z, x)
        for dy in range(1, 4):
            send_tile(0, z, at_y(dy), x)
        got[rows(here * 8), :] = sent[rows(y * 8), :]

    def wait_across():
        half_a, half_b = rows(other * 1024, 1024), rows(other * 512, 512)
        pltpu.make_async_copy(ga.at[half_a], ga.at[half_a], core_recv.at[0]).wait()
        pltpu.make_async_copy(gb.at[half_b], gb.at[half_b], core_recv.at[1]).wait()

    def arrived():
        part = rows(0, 127 * 8)
        pltpu.make_async_copy(got.at[part], got.at[part], go_recv).wait()

        for i in range(16):
            for h in range(2):
                tiles = [got[rows((i * 8 + h * 4 + j) * 8), :] for j in range(4)]
                for k, tile in enumerate(swap_blocks(tiles)):
                    x1[k % 2, rows(i * 16 + (k // 2) * 8), h * 128 : h * 128 + 128] = tile

    steps = dict(
        g=arrived,
        z=wait_z,
        h=wait_halves,
        p=wait_planes,
        tp=tiles_plane,
        t0=functools.partial(tiles_to, 0),
        t1=functools.partial(tiles_to, 1),
        t2=functools.partial(tiles_to, 2),
        t3=functools.partial(tiles_to, 3),
        r0=functools.partial(both, 0, 0),
        r1=functools.partial(both, 0, 1),
        r2=functools.partial(both, 4, 0),
        r3=functools.partial(both, 4, 1),
        c=wait_across,
    )
    for step in ORDER:
        steps[step]()

    def weights(step, c):
        halves = []
        for h in range(2):
            k = step * 4 + c * 2 + h
            halves.append(jnp.concatenate([ga[pl.ds(i * 64 + k, 8, stride=8), :] for i in range(32)], axis=0))
        return jnp.concatenate(halves, axis=1)

    def tail_weights(c):
        halves = []
        for h in range(2):
            blocks = []
            for n in range(8):
                for f in range(2):
                    for j in range(2):
                        start = ((n // 4) * 64 + j * 32 + n % 4) * 8 + f * 4 + c * 2 + h
                        blocks.append(gb[pl.ds(start, 8, stride=32), :])
            halves.append(jnp.concatenate(blocks, axis=0))
        return jnp.concatenate(halves, axis=1)

    for c in range(2):
        for step in range(2):
            wh[step, c], wl[step, c] = split(weights(step, c))
        wh[2, c], wl[2, c] = split(tail_weights(c).T)

    def weight(number, c):
        return wh[number, c], wl[number, c]

    first = product(weight(0, 0), weight(0, 1), split(x1[0]), split(x1[1]))
    second = product(split(first[0]), split(first[1]), weight(2, 0), weight(2, 1))
    y2[0] = second[0]
    y2[1] = second[1]
    for c in range(2):
        for k in range(2):
            for h in range(2):
                for vh in range(2):
                    for jb in range(2):
                        tiles = [
                            y2[c, rows(k * 128 + j * 32 + h * 16 + jb * 8), vh * 128 : vh * 128 + 128] for j in range(4)
                        ]
                        for j, tile in enumerate(swap_blocks(tiles)):
                            zz[c * 2 + h, pl.ds(jb * 128 + k * 8 + vh * 4 + j, 8, stride=16), :] = tile

    def contracted(c):
        return split(jnp.concatenate([zz[c * 2], zz[c * 2 + 1]], axis=1))

    third = product(weight(1, 0), weight(1, 1), contracted(0), contracted(1))
    for c in range(2):
        for k in range(2):
            for h in range(2):
                for i in range(16):
                    back[pl.ds(i * 64 + k * 4 + h * 2 + c, 8, stride=8), :] = third[c][
                        k * 128 + i * 8 : k * 128 + i * 8 + 8, h * 128 : h * 128 + 128
                    ]

    there = (z * 4 + x) * 4 + y

    def half(tile, which):
        return pl.ds(pl.multiple_of(tile * 8 + which * 4, 4), 4)

    def send_back(dz, yt, xt, to_core):
        zt = at_z(dz)
        pltpu.make_async_remote_copy(
            back.at[half((yt * 8 + zt) * 4 + xt, to_core)],
            home.at[half(there, core)],
            back_send,
            back_recv.at[dz & 3],
            device_id=device(zt, yt, xt, to_core),
            device_id_type=MESH,
        ).start()

    for dzs in ((4, 2, 6, 0), (5, 3, 1, 7)):
        for i in range(16):
            for dz in dzs:
                for to_core in (core, other):
                    if i or dz or to_core is other:
                        send_back(dz, at_y(i & 3), at_x(i >> 2), to_core)
    own = pltpu.make_async_copy(
        back.at[half((y * 8 + z) * 4 + x, core)], home.at[half(there, core)], own_sem
    )
    own.start()
    own.wait()

    for j in (0, 2, 1, 3):
        part = rows(0, 256) if j else pl.ds(0, 252)
        pltpu.make_async_copy(home.at[part], home.at[part], back_recv.at[j]).wait()
        zl = (z - j) & 3
        for i in range(4):
            for h in range(2):
                group = (h * 4 + zl) * 4 + i
                tiles = [home[rows((group * 4 + k) * 8), :] for k in range(4)]
                for k, tile in enumerate(swap_blocks(tiles)):
                    for q in range(4):
                        line = (q // 2) * 256 + (zl * 4 + i) * 16 + ((q % 2) * 4 + k) * 2 + h
                        out[pl.ds(line, 2, stride=512), :] = tile[q * 2 : q * 2 + 2]

    part = rows(0, 127 * 8)
    half_a, half_b = rows(core * 1024, 1024), rows(core * 512, 512)
    pltpu.make_async_copy(ga.at[half_a], ga.at[half_a], core_send.at[0]).wait()
    pltpu.make_async_copy(gb.at[half_b], gb.at[half_b], core_send.at[1]).wait()
    pltpu.make_async_copy(ga.at[rows(0, 56)], ga.at[rows(0, 56)], z_send.at[0]).wait()

    @pl.when(gathers_tail)
    def _():
        pltpu.make_async_copy(gb.at[rows(0, 56)], gb.at[rows(0, 56)], z_send.at[1]).wait()

    for one in rings:
        one[2]()
    pltpu.make_async_copy(sent.at[part], sent.at[part], go_send).wait()
    part = pl.ds(0, 1020)
    pltpu.make_async_copy(back.at[part], back.at[part], back_send).wait()


def on_device(stem, branch_pair, branch_last):
    dma = pltpu.SemaphoreType.DMA
    in_hbm = functools.partial(pltpu.with_memory_space_constraint, memory_space=pltpu.HBM)
    whole = pltpu.VMEM((1024, 128), F32)
    result = pl.pallas_call(
        kernel,
        out_shape=pltpu.VMEM((1024, 128), F32),
        in_specs=[
            pl.BlockSpec(memory_space=pltpu.HBM),
            pl.BlockSpec(memory_space=pltpu.HBM),
            pl.BlockSpec(memory_space=pltpu.HBM),
        ],
        out_specs=pl.BlockSpec(memory_space=pltpu.VMEM),
        scratch_shapes=[
            whole,
            whole,
            whole,
            pltpu.VMEM((2, 32, 256), F32),
            pltpu.VMEM((2048, 128), F32),
            whole,
            pltpu.VMEM((3, 2, 256, 256), BF16),
            pltpu.VMEM((3, 2, 256, 256), BF16),
            pltpu.VMEM((2, 256, 256), F32),
            pltpu.VMEM((2, 256, 256), F32),
            pltpu.VMEM((4, 256, 128), F32),
            whole,
            whole,
            pltpu.SemaphoreType.REGULAR,
            dma((2,)),
            dma((2,)),
            dma((2,)),
            dma((2,)),
            dma((2,)),
            dma((2,)),
            dma((8, 3)),
            dma((8, 3)),
            dma((2,)),
            dma((2,)),
            dma,
            dma,
            dma,
            dma((4,)),
            dma,
        ],
        compiler_params=pltpu.CompilerParams(collective_id=0, has_side_effects=True, vmem_limit_bytes=40 << 20),
        name="absorb",
    )(in_hbm(stem.reshape(1024, 128)), in_hbm(branch_pair.reshape(8, 128)), in_hbm(branch_last))
    return result.reshape(stem.shape)


def solution(mesh):
    in_specs = (
        P(None, None, "wide", None, "narrow", None),
        P(None, None, ("wide", "narrow"), None),
        P(None, "narrow", None),
    )
    out_specs = P(None, None, "wide", None, "narrow", None)
    return jax.shard_map(on_device, mesh=mesh, in_specs=in_specs, out_specs=out_specs, check_vma=False)
```

```python
import functools

import jax
import jax.numpy as jnp
from jax import lax
from jax.experimental import pallas as pl
from jax.experimental.pallas import tpu as pltpu
from jax.sharding import PartitionSpec as P

MESH = pl.DeviceIdType.MESH
F32 = jnp.float32
BF16 = jnp.bfloat16
ORDER = ("h", "tp", "z", "r0", "p", "t0", "r1", "t1", "t2", "t3", "r3", "g", "c", "w")


def rows(start, count=8):
    return pl.ds(start if isinstance(start, int) else pl.multiple_of(start, 8), count)


def device(z, y, x, core):
    return ((z & 3) * 8 + x * 2 + core, (z >> 2) * 4 + y)


def swap_blocks(tiles):
    lane = lax.broadcasted_iota(jnp.int32, tiles[0].shape, 1)
    low64 = lane < 64
    low32 = (lane & 32) == 0

    def halves(a, b):
        r = pltpu.roll(jnp.where(low64, b, a), 64, 1)
        return jnp.where(low64, a, r), jnp.where(low64, r, b)

    def quarters(a, b):
        return (
            jnp.where(low32, a, pltpu.roll(b, 32, 1)),
            jnp.where(low32, pltpu.roll(a, 96, 1), b),
        )

    a0, a2 = halves(tiles[0], tiles[2])
    a1, a3 = halves(tiles[1], tiles[3])
    return (*quarters(a0, a1), *quarters(a2, a3))


def split(values):
    high = values.astype(BF16)
    return high, (values - high.astype(F32)).astype(BF16)


def dot(a, b):
    return jnp.dot(a, b, preferred_element_type=F32)


def product(ar, ai, br, bi):
    def left(v):
        return jnp.concatenate([v[0], v[0], v[1]], axis=1)

    def right(v):
        return jnp.concatenate([v[0], v[1], v[0]], axis=0)

    lr, li, rr, ri = left(ar), left(ai), right(br), right(bi)
    return dot(lr, rr) - dot(li, ri), dot(lr, ri) + dot(li, rr)


def kernel(
    stem,
    pair,
    tail,
    out,
    xr,
    sent,
    got,
    tails,
    ga,
    gb,
    wh,
    wl,
    x1,
    y2,
    zz,
    back,
    home,
    plane_sem,
    local_sem,
    branch_sem,
    pair_send,
    pair_recv,
    z_send,
    z_recv,
    ring_send,
    ring_recv,
    core_send,
    core_recv,
    go_send,
    go_recv,
    back_send,
    back_recv,
    own_sem,
):
    wide, narrow = lax.axis_index("wide"), lax.axis_index("narrow")
    core, x = wide & 1, (wide >> 1) & 3
    z, y = (narrow >> 2) * 4 + (wide >> 3), narrow & 3
    other = 1 - core
    sibling = device(z, y, x, other)

    def at_z(d):
        return (z + d) & 7

    def at_x(d):
        return (x + d) & 3

    def at_y(d):
        return (y + d) & 3

    def own_half(c):
        return pltpu.make_async_copy(
            stem.at[rows(c * 512 + core * 256, 256)],
            xr.at[rows(core * 512 + c * 256, 256)],
            local_sem.at[c],
        )

    barrier = pltpu.get_barrier_semaphore()
    for d in (4, 3, 5, 2, 6, 1, 7):
        pl.semaphore_signal(barrier, inc=1, device_id=device(at_z(d), y, x, core), device_id_type=MESH)
    for d in range(1, 16):
        pl.semaphore_signal(
            barrier, inc=1, device_id=device(z, at_y(d // 4), at_x(d % 4), core), device_id_type=MESH
        )
    pl.semaphore_signal(barrier, inc=1, device_id=sibling, device_id_type=MESH)

    slot_a = ((core * 4 + y) * 8 + z) * 4 + x
    slot_b = (z * 4 + x) * 4 + y
    fetches = [
        pltpu.make_async_copy(tail, tails, branch_sem.at[0]),
        pltpu.make_async_copy(pair, ga.at[rows(slot_a * 8)], branch_sem.at[1]),
    ]
    for fetch in fetches:
        fetch.start()
    for c in range(2):
        own_half(c).start()

    for fetch in fetches:
        fetch.wait()
    gathers_tail = (z >> 2) == core

    @pl.when(gathers_tail)
    def _():
        line = lax.broadcasted_iota(jnp.int32, (8, 128), 0)
        pieces = []
        for f in range(2):
            for c in range(2):
                for h in range(2):
                    tile = tails[c, rows(f * 16 + ((z >> 1) & 1) * 8), h * 128 : h * 128 + 128]
                    tile = jnp.where(line == (z & 1) * 4 + x, tile, 0.0)
                    pieces.append(jnp.sum(tile, axis=0, keepdims=True))
        gb[rows(slot_b * 8), :] = jnp.concatenate(pieces, axis=0)

    pl.semaphore_wait(barrier, 23)

    for d in range(1, 8):
        pl.semaphore_signal(plane_sem, inc=1, device_id=device(at_z(d), y, x, core), device_id_type=MESH)

    def half_across(c):
        return pltpu.make_async_remote_copy(
            stem.at[rows(c * 512 + other * 256, 256)],
            xr.at[rows(core * 512 + c * 256, 256)],
            pair_send.at[c],
            pair_recv.at[c],
            device_id=sibling,
            device_id_type=MESH,
        )

    for c in range(2):
        half_across(c).start()

    def along_z(buffer, which, slot, d):
        return pltpu.make_async_remote_copy(
            buffer.at[rows(slot * 8)],
            buffer.at[rows(slot * 8)],
            z_send.at[which],
            z_recv.at[which],
            device_id=device(at_z(d), y, x, core),
            device_id_type=MESH,
        )

    for d in (4, 3, 5, 2, 6, 1, 7):
        along_z(ga, 0, slot_a, d).start()

    @pl.when(gathers_tail)
    def _():
        for d in (4, 3, 5, 2, 6, 1, 7):
            along_z(gb, 1, slot_b, d).start()

    pairs = ga.reshape(2, 4, 2, 4, 4, 8, 128)
    rests = gb.reshape(2, 2, 2, 4, 4, 8, 128)

    def on_x(d):
        return at_x(d), device(z, y, at_x(d), core)

    def on_y(d):
        return at_y(d), device(z, at_y(d), x, core)

    def across(which, ref):
        return pltpu.make_async_remote_copy(
            ref, ref, core_send.at[which], core_recv.at[which], device_id=sibling, device_id_type=MESH
        )

    def ring(number, block, place, which=None):
        def copy(d, holder):
            ref = block(place(holder)[0])
            return pltpu.make_async_remote_copy(
                ref,
                ref,
                ring_send.at[number, d - 1],
                ring_recv.at[number, d - 1],
                device_id=place(d)[1],
                device_id_type=MESH,
            )

        def pass_on(holder):
            if which is not None:
                across(which, block(place(holder)[0])).start()

        def start():
            for d in (2, 1, 3):
                copy(d, 0).start()
            pass_on(0)

        def arrive():
            for d in (1, 3, 2):
                copy(d, -d).wait_recv()
                pass_on(-d)

        def drain():
            for d in (1, 2, 3):
                copy(d, 0).wait_send()

        return start, arrive, drain

    rings = [
        ring(0, lambda p: pairs.at[core, y, 0, :, p], on_x),
        ring(1, lambda p: pairs.at[core, p, 1, :, x], on_y),
        ring(2, lambda p: rests.at[core, 0, :, p, y], on_x),
        ring(3, lambda p: rests.at[core, 1, :, x, p], on_y),
        ring(4, lambda p: pairs.at[core, p, 0], on_y, 0),
        ring(5, lambda p: pairs.at[core, :, 1, :, p], on_x, 0),
        ring(6, lambda p: rests.at[core, 0, :, :, p], on_y, 1),
        ring(7, lambda p: rests.at[core, 1, :, p], on_x, 1),
    ]

    here = (((z & 3) * 4 + x) * 2 + (z >> 2)) * 4 + y

    def shuffle_group(number, zt, xt):
        base = ((zt & 3) * 4 + xt) * 16 + (zt >> 2)
        tiles = [xr[pl.ds(i * 256 + base, 8, stride=2), :] for i in range(4)]
        for j, tile in enumerate(swap_blocks(tiles)):
            sent[rows((number * 4 + j) * 8), :] = tile

    def send_tile(number, zt, yt, xt):
        pltpu.make_async_remote_copy(
            sent.at[rows((number * 4 + yt) * 8)],
            got.at[rows(here * 8)],
            go_send,
            go_recv,
            device_id=device(zt, yt, xt, core),
            device_id_type=MESH,
        ).start()

    def send_groups(dx, dzs):
        for dz in dzs:
            zt, xt = at_z(dz), at_x(dx)
            number = dx * 8 + dz
            shuffle_group(number, zt, xt)
            for dy in range(4):
                send_tile(number, zt, at_y(dy), xt)

    def wait_z():
        part = rows(0, 56)
        pltpu.make_async_copy(ga.at[part], ga.at[part], z_recv.at[0]).wait()

        def wait_tail(count):
            part = rows(0, count * 8)
            pltpu.make_async_copy(gb.at[part], gb.at[part], z_recv.at[1]).wait()

        @pl.when(gathers_tail)
        def _():
            wait_tail(3)

        @pl.when(jnp.logical_not(gathers_tail))
        def _():
            wait_tail(4)

    def wait_halves():
        for c in range(2):
            own_half(c).wait()
        for c in range(2):
            half_across(c).wait()

    def wait_planes():
        pl.semaphore_wait(plane_sem, 7)

    def hand_on():
        for i in range(4):
            rings[i][1]()
            rings[4 + i][0]()

    def both(first, step):
        for one in rings[first : first + 4]:
            one[step]()

    def tiles_to(dx):
        send_groups(dx, (4, 3, 5, 2, 6, 1, 7))

    def tiles_plane():
        send_groups(1, (0,))
        send_groups(2, (0,))
        send_groups(3, (0,))
        shuffle_group(0, z, x)
        for dy in range(1, 4):
            send_tile(0, z, at_y(dy), x)
        got[rows(here * 8), :] = sent[rows(y * 8), :]

    def wait_across():
        half_a, half_b = rows(other * 1024, 1024), rows(other * 512, 512)
        pltpu.make_async_copy(gb.at[half_b], gb.at[half_b], core_recv.at[1]).wait()
        pltpu.make_async_copy(ga.at[half_a], ga.at[half_a], core_recv.at[0]).wait()

    def arrived():
        part = rows(0, 127 * 8)
        pltpu.make_async_copy(got.at[part], got.at[part], go_recv).wait()

        for i in range(16):
            for h in range(2):
                tiles = [got[rows((i * 8 + h * 4 + j) * 8), :] for j in range(4)]
                for k, tile in enumerate(swap_blocks(tiles)):
                    x1[k % 2, rows(i * 16 + (k // 2) * 8), h * 128 : h * 128 + 128] = tile

    def weights(step, c):
        halves = []
        for h in range(2):
            k = step * 4 + c * 2 + h
            halves.append(jnp.concatenate([ga[pl.ds(i * 64 + k, 8, stride=8), :] for i in range(32)], axis=0))
        return jnp.concatenate(halves, axis=1)

    def tail_weights(c):
        halves = []
        for h in range(2):
            blocks = []
            for n in range(8):
                for f in range(2):
                    for j in range(2):
                        start = ((n // 4) * 64 + j * 32 + n % 4) * 8 + f * 4 + c * 2 + h
                        blocks.append(gb[pl.ds(start, 8, stride=32), :])
            halves.append(jnp.concatenate(blocks, axis=0))
        return jnp.concatenate(halves, axis=1)

    def prepare():
        for c in range(2):
            for step in range(2):
                wh[step, c], wl[step, c] = split(weights(step, c))
            wh[2, c], wl[2, c] = split(tail_weights(c).T)

    steps = dict(
        g=arrived,
        w=prepare,
        z=wait_z,
        h=wait_halves,
        p=wait_planes,
        tp=tiles_plane,
        t0=functools.partial(tiles_to, 0),
        t1=functools.partial(tiles_to, 1),
        t2=functools.partial(tiles_to, 2),
        t3=functools.partial(tiles_to, 3),
        r0=functools.partial(both, 0, 0),
        r1=hand_on,
        r3=functools.partial(both, 4, 1),
        c=wait_across,
    )
    for step in ORDER:
        steps[step]()

    def weight(number, c):
        return wh[number, c], wl[number, c]

    first = product(weight(0, 0), weight(0, 1), split(x1[0]), split(x1[1]))
    second = product(split(first[0]), split(first[1]), weight(2, 0), weight(2, 1))
    y2[0] = second[0]
    y2[1] = second[1]
    for c in range(2):
        for k in range(2):
            for h in range(2):
                for vh in range(2):
                    for jb in range(2):
                        tiles = [
                            y2[c, rows(k * 128 + j * 32 + h * 16 + jb * 8), vh * 128 : vh * 128 + 128] for j in range(4)
                        ]
                        for j, tile in enumerate(swap_blocks(tiles)):
                            zz[c * 2 + h, pl.ds(jb * 128 + k * 8 + vh * 4 + j, 8, stride=16), :] = tile

    def contracted(c):
        return split(jnp.concatenate([zz[c * 2], zz[c * 2 + 1]], axis=1))

    third = product(weight(1, 0), weight(1, 1), contracted(0), contracted(1))
    for c in range(2):
        for k in range(2):
            for h in range(2):
                for i in range(16):
                    back[pl.ds(i * 64 + k * 4 + h * 2 + c, 8, stride=8), :] = third[c][
                        k * 128 + i * 8 : k * 128 + i * 8 + 8, h * 128 : h * 128 + 128
                    ]

    there = (z * 4 + x) * 4 + y

    def half(tile, which):
        return pl.ds(pl.multiple_of(tile * 8 + which * 4, 4), 4)

    def send_back(dz, yt, xt, to_core):
        zt = at_z(dz)
        pltpu.make_async_remote_copy(
            back.at[half((yt * 8 + zt) * 4 + xt, to_core)],
            home.at[half(there, core)],
            back_send,
            back_recv.at[dz & 3],
            device_id=device(zt, yt, xt, to_core),
            device_id_type=MESH,
        ).start()

    for dzs in ((4, 2, 6, 0), (5, 3, 1, 7)):
        for i in range(16):
            for dz in dzs:
                for to_core in (core, other):
                    if i or dz or to_core is other:
                        send_back(dz, at_y(i & 3), at_x(i >> 2), to_core)
    own = pltpu.make_async_copy(
        back.at[half((y * 8 + z) * 4 + x, core)], home.at[half(there, core)], own_sem
    )
    own.start()
    own.wait()

    for j in (0, 2, 1, 3):
        part = rows(0, 256) if j else pl.ds(0, 252)
        pltpu.make_async_copy(home.at[part], home.at[part], back_recv.at[j]).wait()
        zl = (z - j) & 3
        for i in range(4):
            for h in range(2):
                group = (h * 4 + zl) * 4 + i
                tiles = [home[rows((group * 4 + k) * 8), :] for k in range(4)]
                for k, tile in enumerate(swap_blocks(tiles)):
                    for q in range(4):
                        line = (q // 2) * 256 + (zl * 4 + i) * 16 + ((q % 2) * 4 + k) * 2 + h
                        out[pl.ds(line, 2, stride=512), :] = tile[q * 2 : q * 2 + 2]

    part = rows(0, 127 * 8)
    half_a, half_b = rows(core * 1024, 1024), rows(core * 512, 512)
    pltpu.make_async_copy(ga.at[half_a], ga.at[half_a], core_send.at[0]).wait()
    pltpu.make_async_copy(gb.at[half_b], gb.at[half_b], core_send.at[1]).wait()
    pltpu.make_async_copy(ga.at[rows(0, 56)], ga.at[rows(0, 56)], z_send.at[0]).wait()

    @pl.when(gathers_tail)
    def _():
        pltpu.make_async_copy(gb.at[rows(0, 56)], gb.at[rows(0, 56)], z_send.at[1]).wait()

    for one in rings:
        one[2]()
    pltpu.make_async_copy(sent.at[part], sent.at[part], go_send).wait()
    part = pl.ds(0, 1020)
    pltpu.make_async_copy(back.at[part], back.at[part], back_send).wait()


def on_device(stem, branch_pair, branch_last):
    dma = pltpu.SemaphoreType.DMA
    in_hbm = functools.partial(pltpu.with_memory_space_constraint, memory_space=pltpu.HBM)
    whole = pltpu.VMEM((1024, 128), F32)
    result = pl.pallas_call(
        kernel,
        out_shape=pltpu.VMEM((1024, 128), F32),
        in_specs=[
            pl.BlockSpec(memory_space=pltpu.HBM),
            pl.BlockSpec(memory_space=pltpu.HBM),
            pl.BlockSpec(memory_space=pltpu.HBM),
        ],
        out_specs=pl.BlockSpec(memory_space=pltpu.VMEM),
        scratch_shapes=[
            whole,
            whole,
            whole,
            pltpu.VMEM((2, 32, 256), F32),
            pltpu.VMEM((2048, 128), F32),
            whole,
            pltpu.VMEM((3, 2, 256, 256), BF16),
            pltpu.VMEM((3, 2, 256, 256), BF16),
            pltpu.VMEM((2, 256, 256), F32),
            pltpu.VMEM((2, 256, 256), F32),
            pltpu.VMEM((4, 256, 128), F32),
            whole,
            whole,
            pltpu.SemaphoreType.REGULAR,
            dma((2,)),
            dma((2,)),
            dma((2,)),
            dma((2,)),
            dma((2,)),
            dma((2,)),
            dma((8, 3)),
            dma((8, 3)),
            dma((2,)),
            dma((2,)),
            dma,
            dma,
            dma,
            dma((4,)),
            dma,
        ],
        compiler_params=pltpu.CompilerParams(collective_id=0, has_side_effects=True, vmem_limit_bytes=40 << 20),
        name="absorb",
    )(in_hbm(stem.reshape(1024, 128)), in_hbm(branch_pair.reshape(8, 128)), in_hbm(branch_last))
    return result.reshape(stem.shape)


def solution(mesh):
    in_specs = (
        P(None, None, "wide", None, "narrow", None),
        P(None, None, ("wide", "narrow"), None),
        P(None, "narrow", None),
    )
    out_specs = P(None, None, "wide", None, "narrow", None)
    return jax.shard_map(on_device, mesh=mesh, in_specs=in_specs, out_specs=out_specs, check_vma=False)
```

```python
import functools

import jax
import jax.numpy as jnp
from jax import lax
from jax.experimental import pallas as pl
from jax.experimental.pallas import tpu as pltpu
from jax.sharding import PartitionSpec as P

MESH = pl.DeviceIdType.MESH
F32 = jnp.float32
BF16 = jnp.bfloat16
ORDER = ("h", "tp", "z", "r0", "p", "t0", "r1", "t1", "t2", "t3", "r3", "g", "c", "w")


def rows(start, count=8):
    return pl.ds(start if isinstance(start, int) else pl.multiple_of(start, 8), count)


def device(z, y, x, core):
    return ((z & 3) * 8 + x * 2 + core, (z >> 2) * 4 + y)


def swap_blocks(tiles):
    lane = lax.broadcasted_iota(jnp.int32, tiles[0].shape, 1)
    low64 = lane < 64
    low32 = (lane & 32) == 0

    def halves(a, b):
        r = pltpu.roll(jnp.where(low64, b, a), 64, 1)
        return jnp.where(low64, a, r), jnp.where(low64, r, b)

    def quarters(a, b):
        return (
            jnp.where(low32, a, pltpu.roll(b, 32, 1)),
            jnp.where(low32, pltpu.roll(a, 96, 1), b),
        )

    a0, a2 = halves(tiles[0], tiles[2])
    a1, a3 = halves(tiles[1], tiles[3])
    return (*quarters(a0, a1), *quarters(a2, a3))


def split(values):
    high = values.astype(BF16)
    return high, (values - high.astype(F32)).astype(BF16)


def dot(a, b):
    return jnp.dot(a, b, preferred_element_type=F32)


def product(ar, ai, br, bi):
    def left(v):
        return jnp.concatenate([v[0], v[0], v[1]], axis=1)

    def right(v):
        return jnp.concatenate([v[0], v[1], v[0]], axis=0)

    lr, li, rr, ri = left(ar), left(ai), right(br), right(bi)
    return dot(lr, rr) - dot(li, ri), dot(lr, ri) + dot(li, rr)


def kernel(
    stem,
    pair,
    tail,
    out,
    xr,
    sent,
    got,
    tails,
    ga,
    gb,
    wh,
    wl,
    x1,
    y2,
    zz,
    back,
    home,
    final,
    plane_sem,
    local_sem,
    branch_sem,
    pair_send,
    pair_recv,
    z_send,
    z_recv,
    ring_send,
    ring_recv,
    core_send,
    core_recv,
    go_send,
    go_recv,
    back_send,
    back_recv,
    here_sem,
    own_sem,
):
    wide, narrow = lax.axis_index("wide"), lax.axis_index("narrow")
    core, x = wide & 1, (wide >> 1) & 3
    z, y = (narrow >> 2) * 4 + (wide >> 3), narrow & 3
    other = 1 - core
    sibling = device(z, y, x, other)

    def at_z(d):
        return (z + d) & 7

    def at_x(d):
        return (x + d) & 3

    def at_y(d):
        return (y + d) & 3

    def own_half(c):
        return pltpu.make_async_copy(
            stem.at[rows(c * 512 + core * 256, 256)],
            xr.at[rows(core * 512 + c * 256, 256)],
            local_sem.at[c],
        )

    barrier = pltpu.get_barrier_semaphore()
    for d in (4, 3, 5, 2, 6, 1, 7):
        pl.semaphore_signal(barrier, inc=1, device_id=device(at_z(d), y, x, core), device_id_type=MESH)
    for d in range(1, 16):
        pl.semaphore_signal(
            barrier, inc=1, device_id=device(z, at_y(d // 4), at_x(d % 4), core), device_id_type=MESH
        )
    pl.semaphore_signal(barrier, inc=1, device_id=sibling, device_id_type=MESH)

    slot_a = ((core * 4 + y) * 8 + z) * 4 + x
    slot_b = (z * 4 + x) * 4 + y
    fetches = [
        pltpu.make_async_copy(tail, tails, branch_sem.at[0]),
        pltpu.make_async_copy(pair, ga.at[rows(slot_a * 8)], branch_sem.at[1]),
    ]
    for fetch in fetches:
        fetch.start()
    for c in range(2):
        own_half(c).start()

    for fetch in fetches:
        fetch.wait()
    gathers_tail = (z >> 2) == core

    @pl.when(gathers_tail)
    def _():
        line = lax.broadcasted_iota(jnp.int32, (8, 128), 0)
        pieces = []
        for f in range(2):
            for c in range(2):
                for h in range(2):
                    tile = tails[c, rows(f * 16 + ((z >> 1) & 1) * 8), h * 128 : h * 128 + 128]
                    tile = jnp.where(line == (z & 1) * 4 + x, tile, 0.0)
                    pieces.append(jnp.sum(tile, axis=0, keepdims=True))
        gb[rows(slot_b * 8), :] = jnp.concatenate(pieces, axis=0)

    pl.semaphore_wait(barrier, 23)

    for d in range(1, 8):
        pl.semaphore_signal(plane_sem, inc=1, device_id=device(at_z(d), y, x, core), device_id_type=MESH)

    def half_across(c):
        return pltpu.make_async_remote_copy(
            stem.at[rows(c * 512 + other * 256, 256)],
            xr.at[rows(core * 512 + c * 256, 256)],
            pair_send.at[c],
            pair_recv.at[c],
            device_id=sibling,
            device_id_type=MESH,
        )

    for c in range(2):
        half_across(c).start()

    def along_z(buffer, which, slot, d):
        return pltpu.make_async_remote_copy(
            buffer.at[rows(slot * 8)],
            buffer.at[rows(slot * 8)],
            z_send.at[which],
            z_recv.at[which],
            device_id=device(at_z(d), y, x, core),
            device_id_type=MESH,
        )

    for d in (4, 3, 5, 2, 6, 1, 7):
        along_z(ga, 0, slot_a, d).start()

    @pl.when(gathers_tail)
    def _():
        for d in (4, 3, 5, 2, 6, 1, 7):
            along_z(gb, 1, slot_b, d).start()

    pairs = ga.reshape(2, 4, 2, 4, 4, 8, 128)
    rests = gb.reshape(2, 2, 2, 4, 4, 8, 128)

    def on_x(d):
        return at_x(d), device(z, y, at_x(d), core)

    def on_y(d):
        return at_y(d), device(z, at_y(d), x, core)

    def across(which, ref):
        return pltpu.make_async_remote_copy(
            ref, ref, core_send.at[which], core_recv.at[which], device_id=sibling, device_id_type=MESH
        )

    def ring(number, block, place, which=None):
        def copy(d, holder):
            ref = block(place(holder)[0])
            return pltpu.make_async_remote_copy(
                ref,
                ref,
                ring_send.at[number, d - 1],
                ring_recv.at[number, d - 1],
                device_id=place(d)[1],
                device_id_type=MESH,
            )

        def pass_on(holder):
            if which is not None:
                across(which, block(place(holder)[0])).start()

        def start():
            for d in (2, 1, 3):
                copy(d, 0).start()
            pass_on(0)

        def arrive():
            for d in (1, 3, 2):
                copy(d, -d).wait_recv()
                pass_on(-d)

        def drain():
            for d in (1, 2, 3):
                copy(d, 0).wait_send()

        return start, arrive, drain

    rings = [
        ring(0, lambda p: pairs.at[core, y, 0, :, p], on_x),
        ring(1, lambda p: pairs.at[core, p, 1, :, x], on_y),
        ring(2, lambda p: rests.at[core, 0, :, p, y], on_x),
        ring(3, lambda p: rests.at[core, 1, :, x, p], on_y),
        ring(4, lambda p: pairs.at[core, p, 0], on_y, 0),
        ring(5, lambda p: pairs.at[core, :, 1, :, p], on_x, 0),
        ring(6, lambda p: rests.at[core, 0, :, :, p], on_y, 1),
        ring(7, lambda p: rests.at[core, 1, :, p], on_x, 1),
    ]

    here = (((z & 3) * 4 + x) * 2 + (z >> 2)) * 4 + y

    def shuffle_group(number, zt, xt):
        base = ((zt & 3) * 4 + xt) * 16 + (zt >> 2)
        tiles = [xr[pl.ds(i * 256 + base, 8, stride=2), :] for i in range(4)]
        for j, tile in enumerate(swap_blocks(tiles)):
            sent[rows((number * 4 + j) * 8), :] = tile

    def send_tile(number, zt, yt, xt):
        pltpu.make_async_remote_copy(
            sent.at[rows((number * 4 + yt) * 8)],
            got.at[rows(here * 8)],
            go_send,
            go_recv,
            device_id=device(zt, yt, xt, core),
            device_id_type=MESH,
        ).start()

    def send_groups(dx, dzs):
        for dz in dzs:
            zt, xt = at_z(dz), at_x(dx)
            number = dx * 8 + dz
            shuffle_group(number, zt, xt)
            for dy in range(4):
                send_tile(number, zt, at_y(dy), xt)

    def wait_z():
        part = rows(0, 56)
        pltpu.make_async_copy(ga.at[part], ga.at[part], z_recv.at[0]).wait()

        def wait_tail(count):
            part = rows(0, count * 8)
            pltpu.make_async_copy(gb.at[part], gb.at[part], z_recv.at[1]).wait()

        @pl.when(gathers_tail)
        def _():
            wait_tail(3)

        @pl.when(jnp.logical_not(gathers_tail))
        def _():
            wait_tail(4)

    def wait_halves():
        for c in range(2):
            own_half(c).wait()
        for c in range(2):
            half_across(c).wait()

    def wait_planes():
        pl.semaphore_wait(plane_sem, 7)

    def hand_on():
        for i in range(4):
            rings[i][1]()
            rings[4 + i][0]()

    def both(first, step):
        for one in rings[first : first + 4]:
            one[step]()

    def tiles_to(dx):
        send_groups(dx, (4, 3, 5, 2, 6, 1, 7))

    def tiles_plane():
        send_groups(1, (0,))
        send_groups(2, (0,))
        send_groups(3, (0,))
        shuffle_group(0, z, x)
        for dy in range(1, 4):
            send_tile(0, z, at_y(dy), x)
        got[rows(here * 8), :] = sent[rows(y * 8), :]

    def wait_across():
        half_a, half_b = rows(other * 1024, 1024), rows(other * 512, 512)
        pltpu.make_async_copy(gb.at[half_b], gb.at[half_b], core_recv.at[1]).wait()
        pltpu.make_async_copy(ga.at[half_a], ga.at[half_a], core_recv.at[0]).wait()

    def arrived():
        part = rows(0, 127 * 8)
        pltpu.make_async_copy(got.at[part], got.at[part], go_recv).wait()

        for i in range(16):
            for h in range(2):
                tiles = [got[rows((i * 8 + h * 4 + j) * 8), :] for j in range(4)]
                for k, tile in enumerate(swap_blocks(tiles)):
                    x1[k % 2, rows(i * 16 + (k // 2) * 8), h * 128 : h * 128 + 128] = tile

    def weights(step, c):
        halves = []
        for h in range(2):
            k = step * 4 + c * 2 + h
            halves.append(jnp.concatenate([ga[pl.ds(i * 64 + k, 8, stride=8), :] for i in range(32)], axis=0))
        return jnp.concatenate(halves, axis=1)

    def tail_weights(c):
        halves = []
        for h in range(2):
            blocks = []
            for n in range(8):
                for f in range(2):
                    for j in range(2):
                        start = ((n // 4) * 64 + j * 32 + n % 4) * 8 + f * 4 + c * 2 + h
                        blocks.append(gb[pl.ds(start, 8, stride=32), :])
            halves.append(jnp.concatenate(blocks, axis=0))
        return jnp.concatenate(halves, axis=1)

    def prepare():
        for c in range(2):
            for step in range(2):
                wh[step, c], wl[step, c] = split(weights(step, c))
            wh[2, c], wl[2, c] = split(tail_weights(c).T)

    steps = dict(
        g=arrived,
        w=prepare,
        z=wait_z,
        h=wait_halves,
        p=wait_planes,
        tp=tiles_plane,
        t0=functools.partial(tiles_to, 0),
        t1=functools.partial(tiles_to, 1),
        t2=functools.partial(tiles_to, 2),
        t3=functools.partial(tiles_to, 3),
        r0=functools.partial(both, 0, 0),
        r1=hand_on,
        r3=functools.partial(both, 4, 1),
        c=wait_across,
    )
    for step in ORDER:
        steps[step]()

    def weight(number, c):
        return wh[number, c], wl[number, c]

    first = product(weight(0, 0), weight(0, 1), split(x1[0]), split(x1[1]))
    second = product(split(first[0]), split(first[1]), weight(2, 0), weight(2, 1))
    y2[0] = second[0]
    y2[1] = second[1]
    for c in range(2):
        for k in range(2):
            for h in range(2):
                for vh in range(2):
                    for jb in range(2):
                        tiles = [
                            y2[c, rows(k * 128 + j * 32 + h * 16 + jb * 8), vh * 128 : vh * 128 + 128] for j in range(4)
                        ]
                        for j, tile in enumerate(swap_blocks(tiles)):
                            zz[c * 2 + h, pl.ds(jb * 128 + k * 8 + vh * 4 + j, 8, stride=16), :] = tile

    def contracted(c):
        return split(jnp.concatenate([zz[c * 2], zz[c * 2 + 1]], axis=1))

    third = product(weight(1, 0), weight(1, 1), contracted(0), contracted(1))
    for c in range(2):
        for k in range(2):
            for h in range(2):
                for i in range(16):
                    back[pl.ds(i * 64 + k * 4 + h * 2 + c, 8, stride=8), :] = third[c][
                        k * 128 + i * 8 : k * 128 + i * 8 + 8, h * 128 : h * 128 + 128
                    ]

    there = (z * 4 + x) * 4 + y

    def half(tile, which):
        return pl.ds(pl.multiple_of(tile * 8 + which * 4, 4), 4)

    def send_back(dz, yt, xt, to_core):
        zt = at_z(dz)
        pltpu.make_async_remote_copy(
            back.at[half((yt * 8 + zt) * 4 + xt, to_core)],
            home.at[half(there, core)],
            back_send,
            back_recv.at[dz & 3],
            device_id=device(zt, yt, xt, to_core),
            device_id_type=MESH,
        ).start()

    for dzs in ((4, 2, 6, 0), (5, 3, 1, 7)):
        for i in range(16):
            for dz in dzs:
                for to_core in (core, other):
                    if i or dz or to_core is other:
                        send_back(dz, at_y(i & 3), at_x(i >> 2), to_core)
    own = pltpu.make_async_copy(
        back.at[half((y * 8 + z) * 4 + x, core)], home.at[half(there, core)], own_sem
    )
    own.start()
    own.wait()

    parts = out.reshape(2, 2, 4, 4, 2, 8, 128)
    for j in (0, 2, 1, 3):
        part = rows(0, 256) if j else pl.ds(0, 252)
        pltpu.make_async_copy(home.at[part], home.at[part], back_recv.at[j]).wait()
        zl = (z - j) & 3
        for i in range(4):
            for h in range(2):
                group = (h * 4 + zl) * 4 + i
                tiles = [home[rows((group * 4 + k) * 8), :] for k in range(4)]
                for k, tile in enumerate(swap_blocks(tiles)):
                    final[pl.ds((zl * 4 + i) * 8 + k * 2 + h, 8, stride=128), :] = tile
        for k in range(8):
            pltpu.make_async_copy(
                final.reshape(8, 4, 4, 8, 128).at[k, zl],
                parts.at[k % 2, k // 4, zl, :, (k // 2) % 2],
                here_sem,
            ).start()

    part = rows(0, 127 * 8)
    half_a, half_b = rows(core * 1024, 1024), rows(core * 512, 512)
    pltpu.make_async_copy(ga.at[half_a], ga.at[half_a], core_send.at[0]).wait()
    pltpu.make_async_copy(gb.at[half_b], gb.at[half_b], core_send.at[1]).wait()
    pltpu.make_async_copy(ga.at[rows(0, 56)], ga.at[rows(0, 56)], z_send.at[0]).wait()

    @pl.when(gathers_tail)
    def _():
        pltpu.make_async_copy(gb.at[rows(0, 56)], gb.at[rows(0, 56)], z_send.at[1]).wait()

    for one in rings:
        one[2]()
    pltpu.make_async_copy(sent.at[part], sent.at[part], go_send).wait()
    part = pl.ds(0, 1020)
    pltpu.make_async_copy(back.at[part], back.at[part], back_send).wait()
    pltpu.make_async_copy(final, final, here_sem).wait()


def on_device(stem, branch_pair, branch_last):
    dma = pltpu.SemaphoreType.DMA
    in_hbm = functools.partial(pltpu.with_memory_space_constraint, memory_space=pltpu.HBM)
    whole = pltpu.VMEM((1024, 128), F32)
    result = pl.pallas_call(
        kernel,
        out_shape=pltpu.VMEM((1024, 128), F32),
        in_specs=[
            pl.BlockSpec(memory_space=pltpu.HBM),
            pl.BlockSpec(memory_space=pltpu.HBM),
            pl.BlockSpec(memory_space=pltpu.HBM),
        ],
        out_specs=pl.BlockSpec(memory_space=pltpu.VMEM),
        scratch_shapes=[
            whole,
            whole,
            whole,
            pltpu.VMEM((2, 32, 256), F32),
            pltpu.VMEM((2048, 128), F32),
            whole,
            pltpu.VMEM((3, 2, 256, 256), BF16),
            pltpu.VMEM((3, 2, 256, 256), BF16),
            pltpu.VMEM((2, 256, 256), F32),
            pltpu.VMEM((2, 256, 256), F32),
            pltpu.VMEM((4, 256, 128), F32),
            whole,
            whole,
            whole,
            pltpu.SemaphoreType.REGULAR,
            dma((2,)),
            dma((2,)),
            dma((2,)),
            dma((2,)),
            dma((2,)),
            dma((2,)),
            dma((8, 3)),
            dma((8, 3)),
            dma((2,)),
            dma((2,)),
            dma,
            dma,
            dma,
            dma((4,)),
            dma,
            dma,
        ],
        compiler_params=pltpu.CompilerParams(collective_id=0, has_side_effects=True, vmem_limit_bytes=40 << 20),
        name="absorb",
    )(in_hbm(stem.reshape(1024, 128)), in_hbm(branch_pair.reshape(8, 128)), in_hbm(branch_last))
    return result.reshape(stem.shape)


def solution(mesh):
    in_specs = (
        P(None, None, "wide", None, "narrow", None),
        P(None, None, ("wide", "narrow"), None),
        P(None, "narrow", None),
    )
    out_specs = P(None, None, "wide", None, "narrow", None)
    return jax.shard_map(on_device, mesh=mesh, in_specs=in_specs, out_specs=out_specs, check_vma=False)
```
